512 devices in a mesh: blk: 16 (over x, z_hi, core), head: 32 (over y, z_lo).
Axes of the slice: x: 4, y: 4, z: 16 (z_hi: 2, z_lo: 8; z = z_hi * 8 + z_lo), core: 2. Of those that a mesh axis runs over, the one named last changes fastest.
Arguments:
- queries: bfloat16 [16, 32, 256, 128], P('blk', 'head'), may hold values from -24 to 24
- keys: bfloat16 [16, 32, 256, 128], P('blk', 'head'), may hold values from -6 to 6
- values: bfloat16 [16, 32, 256, 128], P('blk', 'head'), may hold values from -6 to 6
- grad_out: bfloat16 [16, 32, 256, 128], P('blk', 'head'), may hold values from -384 to 384
- key_tiles: int32 [64, 32], replicated, may hold values from 0 to 64, as said below
- work_lists: int32 [16, 32, 2], replicated, may hold values from 0 to 3, as said below
Outputs:
- grad_queries: bfloat16 [16, 32, 256, 128], P('blk', 'head')
- grad_keys: bfloat16 [16, 32, 256, 128], P('blk', 'head')
- grad_values: bfloat16 [16, 32, 256, 128], P('blk', 'head')
The draws below stay inside these ranges and needn't reach their ends.
Inputs may be any that keep to these rules, and one draw needn't show every extreme that they name: `key_tiles`: each row lists distinct key tiles in rising order, always its own tile, then is filled up with 64; a row lists at most 32 tiles, and the first tile of every section lists exactly 32. `work_lists`: for each section and head n, the lists of slots 2 n and 2 n + 1 together hold each of the section's 4 tiles once.
All inputs are finite; a program needn't handle non-finite values.
Results may differ from the reference program's by a relative error of at most 0.018.
Values may be sent and summed in bfloat16 or wider, within the bound.
No kernel may reach another device: no remote copies, remote signals or barrier semaphores. Data moves between devices by JAX's collectives and lax.ppermute only.
A program may use at most 64 MiB of HBM per device.

```python
import jax
import jax.numpy as jnp
from jax import lax

HD = 128
HEADS = 16
TILE = 128
TS_DEV = 2
TS = 4
HALF = 256
NQT = 64
TOKENS = 8192
NNB = 32
N_BLK = 16


def draw_queries(key, part):
    own_key = jax.random.fold_in(key, 11)
    drawn = jnp.clip(jax.random.normal(own_key, (N_BLK, 2 * HEADS, HALF, HD), jnp.float32), -6.0, 6.0)
    return drawn.astype(jnp.bfloat16)


def draw_keys(key, part):
    own_key = jax.random.fold_in(key, 23)
    drawn = jnp.clip(jax.random.normal(own_key, (N_BLK, 2 * HEADS, HALF, HD), jnp.float32), -6.0, 6.0)
    return drawn.astype(jnp.bfloat16)


def draw_key_tiles(key, part):
    own_key = jax.random.fold_in(key, 37)
    first_key, second_key = jax.random.split(own_key)
    tile_ids = jnp.arange(NQT).astype(jnp.int32)
    section_of = tile_ids // TS
    distance = jnp.abs(section_of[:, None] - section_of[None, :])
    raw = jax.random.randint(first_key, (NQT, NQT), 0, 65536)
    ranking = jnp.right_shift(raw, jnp.minimum(distance, 15)) * NQT + tile_ids[None, :]
    ranking = jnp.where(tile_ids[:, None] == tile_ids[None, :], 65536 * NQT + tile_ids[None, :], ranking)
    chosen = lax.top_k(ranking, NNB)[1].astype(jnp.int32)
    counts = jax.random.randint(second_key, (NQT,), NNB // 2, NNB + 1)
    counts = jnp.where(tile_ids % TS == 0, NNB, counts)
    keep = jnp.arange(NNB)[None, :] < counts[:, None]
    listed = jnp.where(keep, chosen, NQT)
    return jnp.sort(listed, axis=1).astype(jnp.int32)


def draw_work_lists(key, part):
    own_key = jax.random.fold_in(key, 53)
    raw = jax.random.randint(own_key, (N_BLK, HEADS, TS), 0, 1048576)
    order = jnp.argsort(raw * TS + jnp.arange(TS)[None, None, :], axis=2)
    return order.reshape(N_BLK, 2 * HEADS, TS_DEV).astype(jnp.int32)


def levels(stream_key, dims, cuts, low, top_value):
    def one(axis_at, blocks):
        draws = jax.random.uniform(jax.random.fold_in(jax.random.fold_in(stream_key, 6), axis_at), (blocks,), jnp.float32, low / len(cuts), top_value / len(cuts))
        return jnp.repeat(jnp.exp(draws), dims[axis_at] // blocks).reshape((-1,) + (1,) * (len(dims) - axis_at - 1))

    level = one(*cuts[0])
    for cut in cuts[1:]:
        level = level * one(*cut)
    return level


def gaussian(key, dims, spread, most, pieces=(), kind=jnp.bfloat16):
    values = jax.random.normal(key, dims, jnp.float32) * spread
    if len(pieces) > 0:
        values = levels(key, dims, pieces, -0.22, 0.18) * values
    return jnp.clip(values, min=-most, max=most).astype(kind)


def setup_inputs(seed: int = 0) -> dict:
    seeds = jax.random.split(jax.random.key(seed), 7)
    queries = draw_queries(jax.random.fold_in(seeds[6], 71), 0)
    keys = draw_keys(jax.random.fold_in(seeds[6], 71), 0)
    values = gaussian(seeds[2], (N_BLK, 2 * HEADS, HALF, HD), 1.0, 6.0, ((0, 16), (1, 32)))
    grad_out = gaussian(seeds[3], (N_BLK, 2 * HEADS, HALF, HD), 64.0, 384.0, ((0, 16), (1, 32)))
    key_tiles = draw_key_tiles(jax.random.fold_in(seeds[6], 71), 0)
    work_lists = draw_work_lists(jax.random.fold_in(seeds[6], 71), 0)
    return dict(queries=queries, keys=keys, values=values, grad_out=grad_out, key_tiles=key_tiles, work_lists=work_lists)


def to_heads(array):
    shaped = array.reshape(N_BLK, HEADS, 2, HALF, HD)
    shaped = jnp.transpose(shaped, (1, 0, 2, 3, 4))
    return shaped.reshape(HEADS, TOKENS, HD)


def from_heads(array):
    shaped = array.reshape(HEADS, N_BLK, 2, HALF, HD)
    shaped = jnp.transpose(shaped, (1, 0, 2, 3, 4))
    return shaped.reshape(N_BLK, 2 * HEADS, HALF, HD)


def one_head(operands, allowed):
    query_rows, key_rows, value_rows, grad_rows = operands
    softmax_scale = HD ** -0.5
    scores = jnp.dot(query_rows, key_rows.T, preferred_element_type=jnp.float32) * softmax_scale
    row_top = jnp.max(jnp.where(allowed, scores, -1e30), axis=1, keepdims=True)
    weights = jnp.where(allowed, jnp.exp(scores - row_top), 0.0)
    log_norm = row_top + jnp.log(jnp.sum(weights, axis=1, keepdims=True))
    probability = jnp.where(allowed, jnp.exp(scores - log_norm), 0.0)
    attended = jnp.dot(probability, value_rows.astype(jnp.float32), precision=lax.Precision.HIGHEST)
    delta_rows = jnp.sum(grad_rows.astype(jnp.float32) * attended, axis=1, keepdims=True)
    probs_b = probability.astype(jnp.bfloat16)
    grad_v = jnp.dot(probs_b.T, grad_rows, preferred_element_type=jnp.float32)
    grad_probs = jnp.dot(grad_rows, value_rows.T, preferred_element_type=jnp.float32)
    grad_scores = (probability * (grad_probs - delta_rows)).astype(jnp.bfloat16)
    grad_q = jnp.dot(grad_scores, key_rows, preferred_element_type=jnp.float32) * softmax_scale
    grad_k = jnp.dot(grad_scores.T, query_rows, preferred_element_type=jnp.float32) * softmax_scale
    return grad_q, grad_k, grad_v


def reference(queries, keys, values, grad_out, key_tiles, work_lists):
    tile_ids = jnp.arange(NQT).astype(jnp.int32)
    tile_allowed = jnp.any(key_tiles[:, :, None] == tile_ids[None, None, :], axis=1)
    allowed = jnp.repeat(jnp.repeat(tile_allowed, TILE, axis=0), TILE, axis=1)
    operands = (to_heads(queries), to_heads(keys), to_heads(values), to_heads(grad_out))
    grad_q, grad_k, grad_v = lax.map(lambda item: one_head(item, allowed), operands)
    by_tile = grad_q.reshape(HEADS, N_BLK, TS, TILE, HD)
    section_idx = jnp.arange(N_BLK).astype(jnp.int32)[:, None, None]
    head_idx = (jnp.arange(2 * HEADS).astype(jnp.int32) // 2)[None, :, None]
    picked = by_tile[head_idx, section_idx, work_lists]
    grad_queries = picked.reshape(N_BLK, 2 * HEADS, HALF, HD).astype(jnp.bfloat16)
    return grad_queries, from_heads(grad_k).astype(jnp.bfloat16), from_heads(grad_v).astype(jnp.bfloat16)
```

```python
import functools

import jax
import jax.numpy as jnp
from jax import lax
from jax.experimental import pallas as pl
from jax.experimental.pallas import tpu as pltpu
from jax.sharding import Mesh, PartitionSpec as P

TILE = 128
HD = 128
HALF = 256
NX = 4
NCHUNK = 4
BLOCKS = 2 * NX
ROWS = BLOCKS * HALF
SCALE = HD**-0.5
SCALE2 = SCALE * 1.4426950408889634
FAR = 1e30


def dot_t(a, b):
    return lax.dot_general(a, b, (((1,), (1,)), ((), ())), preferred_element_type=jnp.float32)


def dot_n(a, b):
    return jnp.dot(a, b, preferred_element_type=jnp.float32)


def mask_kernel(tiles_ref, across_ref, far_ref, live_ref, same_ref, table_ref):
    x, zh, core, half = (lax.axis_index(name) for name in ("x", "zh", "c", "p"))
    tiles = tiles_ref[...]
    for k in range(2 * NCHUNK):
        chunk_zh = zh if k // 2 % 2 == 0 else 1 - zh
        chunk_core = core if k // 4 == 0 else 1 - core
        key_id = (4 * x + 2 * chunk_zh + chunk_core) * 4 + 2 * half + k % 2
        hit = jnp.where(tiles == key_id, 0.0, FAR)
        table_ref[k] = jnp.broadcast_to(jnp.min(hit, axis=1, keepdims=True), (64, TILE))
    for n in range(NX):
        first = (4 * n + 2 * zh + core) * 4
        nearest = jnp.full((4, TILE), FAR, jnp.float32)
        for k in range(2 * NCHUNK):
            four = table_ref[k, pl.ds(first, 4), :]
            nearest = jnp.minimum(nearest, four)
            for h in range(2):
                far_ref[n, h, k : k + 1, :TILE] = four[2 * h : 2 * h + 1]
                far_ref[n, h, k : k + 1, TILE:] = four[2 * h + 1 : 2 * h + 2]
        live_ref[n] = (jnp.min(nearest) < 1.0).astype(jnp.int32)


def stats_kernel(
    live_ref, qg_ref, own_ref, across_ref, core_ref, core_across_ref, far_ref, out_ref
):
    chunks = (own_ref, across_ref, core_ref, core_across_ref)

    def group(n, carry):
        @pl.when(live_ref[n] > 0)
        def _():
            for h in range(2):
                q = qg_ref[n, h, 0]
                g = qg_ref[n, h, 1]
                far = far_ref[n, h]
                scores = []
                top = jnp.full((1, HALF), -FAR, jnp.float32)
                for i, chunk in enumerate(chunks):
                    s = dot_t(chunk[0], q)
                    for t in range(2):
                        st = s[t * TILE : (t + 1) * TILE]
                        scores.append(st)
                        k = 2 * i + t
                        near = jnp.max(st, axis=0, keepdims=True) - far[k : k + 1]
                        top = jnp.maximum(top, near)
                top = top * SCALE2
                total = jnp.zeros((1, HALF), jnp.float32)
                weighted = jnp.zeros((1, HALF), jnp.float32)
                for i, chunk in enumerate(chunks):
                    gp = dot_t(chunk[1], g)
                    for t in range(2):
                        k = 2 * i + t
                        e = jnp.exp2(scores[k] * SCALE2 - (top + 4.0 * far[k : k + 1]))
                        total = total + jnp.sum(e, axis=0, keepdims=True)
                        weighted = weighted + jnp.sum(
                            e * gp[t * TILE : (t + 1) * TILE], axis=0, keepdims=True
                        )
                some = total > 0.0
                safe = jnp.where(some, total, 1.0)
                lse = jnp.where(some, top + jnp.log2(safe), -FAR)
                mean = jnp.where(some, weighted / safe, 0.0)
                for j in range(BLOCKS):
                    out_ref[j, n, h, :, :HALF] = lse
                    out_ref[j, n, h, :, HALF:] = mean

        @pl.when(live_ref[n] == 0)
        def _():
            for j in range(BLOCKS):
                for h in range(2):
                    out_ref[j, n, h, :, :HALF] = jnp.full((1, HALF), -FAR, jnp.float32)
                    out_ref[j, n, h, :, HALF:] = jnp.zeros((1, HALF), jnp.float32)

        return carry

    lax.fori_loop(0, NX, group, 0)


def grads_kernel(
    live_ref,
    work_ref,
    qg_ref,
    own_ref,
    across_ref,
    core_ref,
    core_across_ref,
    far_ref,
    stats_ref,
    keep_ref,
    send_ref,
    dq_ref,
    dk_acc,
    dv_acc,
    kt_ref,
    ds_ref,
):
    zh, core, head = (lax.axis_index(name) for name in ("zh", "c", "n"))
    chunks = (own_ref, across_ref, core_ref, core_across_ref)
    dk_acc[...] = jnp.zeros_like(dk_acc)
    dv_acc[...] = jnp.zeros_like(dv_acc)
    for i, chunk in enumerate(chunks):
        kt_ref[:, i * HALF : (i + 1) * HALF] = chunk[0].T

    def group(n, carry):
        section = 4 * n + 2 * zh + core

        def slot(wanted):
            found = jnp.int32(3)
            for w in range(3):
                found = jnp.where(work_ref[section, 4 * head + w] == wanted, w, found)
            return found

        @pl.when(live_ref[n] > 0)
        def _():
            q_all = qg_ref[n, :, 0].reshape(2 * HALF, HD)
            g_all = qg_ref[n, :, 1].reshape(2 * HALF, HD)
            rows_stats = []
            for h in range(2):
                lse_parts = [stats_ref[j, n, h, :, :HALF] for j in range(BLOCKS)]
                top = functools.reduce(jnp.maximum, lse_parts)
                total = jnp.zeros((1, HALF), jnp.float32)
                weighted = jnp.zeros((1, HALF), jnp.float32)
                for j in range(BLOCKS):
                    w = jnp.exp2(lse_parts[j] - top)
                    total = total + w
                    weighted = weighted + w * stats_ref[j, n, h, :, HALF:]
                rows_stats.append((top + jnp.log2(total), weighted / total))
            for i, chunk in enumerate(chunks):
                rows = slice(i * HALF, (i + 1) * HALF)
                ps, ds = [], []
                for h in range(2):
                    lse, delta = rows_stats[h]
                    s = dot_t(chunk[0], qg_ref[n, h, 0])
                    gp = dot_t(chunk[1], qg_ref[n, h, 1])
                    p_parts, d_parts = [], []
                    for t in range(2):
                        k = 2 * i + t
                        part = slice(t * TILE, (t + 1) * TILE)
                        shift = lse + 4.0 * far_ref[n, h, k : k + 1, :]
                        p = jnp.exp2(s[part] * SCALE2 - shift)
                        p_parts.append(p.astype(jnp.bfloat16))
                        d_parts.append((p * (gp[part] - delta)).astype(jnp.bfloat16))
                    ps.append(jnp.concatenate(p_parts, axis=0))
                    d = jnp.concatenate(d_parts, axis=0)
                    ds.append(d)
                    ds_ref[h, rows] = d
                dv_acc[rows] += dot_n(jnp.concatenate(ps, axis=1), g_all)
                dk_acc[rows] += dot_n(jnp.concatenate(ds, axis=1), q_all)
            for h in range(2):
                dq = (dot_n(kt_ref[...], ds_ref[h]) * SCALE).T.astype(jnp.bfloat16)
                dq_ref[n, slot(2 * h)] = dq[:TILE]
                dq_ref[n, slot(2 * h + 1)] = dq[TILE:]

        @pl.when(live_ref[n] == 0)
        def _():
            dq_ref[n] = jnp.zeros((4, TILE, HD), jnp.bfloat16)

        return carry

    lax.fori_loop(0, NX, group, 0)
    for i in range(2):
        rows = slice(i * HALF, (i + 1) * HALF)
        keep_ref[i, 0] = dk_acc[rows] * SCALE
        keep_ref[i, 1] = dv_acc[rows]
        rows = slice((i + 2) * HALF, (i + 3) * HALF)
        send_ref[i, 0] = (dk_acc[rows] * SCALE).astype(jnp.bfloat16)
        send_ref[i, 1] = dv_acc[rows].astype(jnp.bfloat16)


VMEM = pl.BlockSpec(memory_space=pltpu.VMEM)
SMEM = pl.BlockSpec(memory_space=pltpu.SMEM)


def flipped(value, axis):
    return lax.ppermute(value, axis, [(0, 1), (1, 0)])


def run_masks(tiles, across):
    return pl.pallas_call(
        mask_kernel,
        out_shape=[
            jax.ShapeDtypeStruct((NX, 2, 2 * NCHUNK, HALF), jnp.float32),
            jax.ShapeDtypeStruct((NX,), jnp.int32),
            jax.ShapeDtypeStruct(across.shape, across.dtype),
        ],
        in_specs=[VMEM, pl.BlockSpec(memory_space=pl.ANY)],
        out_specs=[VMEM, SMEM, pl.BlockSpec(memory_space=pl.ANY)],
        input_output_aliases={1: 2},
        scratch_shapes=[pltpu.VMEM((2 * NCHUNK, 64, TILE), jnp.float32)],
        compiler_params=pltpu.CompilerParams(vmem_limit_bytes=8 * 1024 * 1024),
        cost_estimate=pl.CostEstimate(flops=10**11, bytes_accessed=2**20, transcendentals=0),
        name="masks",
    )(tiles, across)


def run_stats(live, qg, kv, far):
    return pl.pallas_call(
        stats_kernel,
        out_shape=jax.ShapeDtypeStruct((BLOCKS, NX, 2, 1, 2 * HALF), jnp.float32),
        in_specs=[SMEM] + [VMEM] * 6,
        out_specs=VMEM,
        compiler_params=pltpu.CompilerParams(vmem_limit_bytes=32 * 1024 * 1024),
        cost_estimate=pl.CostEstimate(flops=10**9, bytes_accessed=2**21, transcendentals=2**21),
        name="stats",
    )(live, qg, *kv, far)


def run_grads(live, work, qg, kv, far, stats):
    return pl.pallas_call(
        grads_kernel,
        out_shape=[
            jax.ShapeDtypeStruct((2, 2, HALF, HD), jnp.float32),
            jax.ShapeDtypeStruct((2, 2, HALF, HD), jnp.bfloat16),
            jax.ShapeDtypeStruct((NX, 4, TILE, HD), jnp.bfloat16),
        ],
        in_specs=[SMEM, SMEM] + [VMEM] * 7,
        out_specs=[VMEM] * 3,
        scratch_shapes=[
            pltpu.VMEM((NCHUNK * HALF, HD), jnp.float32),
            pltpu.VMEM((NCHUNK * HALF, HD), jnp.float32),
            pltpu.VMEM((HD, NCHUNK * HALF), jnp.bfloat16),
            pltpu.VMEM((2, NCHUNK * HALF, HALF), jnp.bfloat16),
        ],
        compiler_params=pltpu.CompilerParams(vmem_limit_bytes=24 * 1024 * 1024),
        cost_estimate=pl.CostEstimate(flops=2 * 10**9, bytes_accessed=2**21, transcendentals=2**21),
        name="grads",
    )(live, work, qg, *kv, far, stats)


def finish_kernel(mine_ref, across_ref, dk_ref, dv_ref):
    dk_ref[...] = (mine_ref[0] + across_ref[0].astype(jnp.float32)).astype(jnp.bfloat16)
    dv_ref[...] = (mine_ref[1] + across_ref[1].astype(jnp.float32)).astype(jnp.bfloat16)


def run_finish(mine, across):
    return pl.pallas_call(
        finish_kernel,
        out_shape=[jax.ShapeDtypeStruct((HALF, HD), jnp.bfloat16)] * 2,
        in_specs=[VMEM, VMEM],
        out_specs=[VMEM, VMEM],
        compiler_params=pltpu.CompilerParams(vmem_limit_bytes=8 * 1024 * 1024),
        cost_estimate=pl.CostEstimate(flops=10**11, bytes_accessed=2**20, transcendentals=0),
        name="finish",
    )(mine, across)


def on_device(queries, keys, values, grad_out, key_tiles, work_lists):
    own_qg = jnp.stack([queries[0, 0], grad_out[0, 0]])
    both_qg = lax.all_gather(own_qg, "p")
    own_kv = jnp.stack([keys[0, 0], values[0, 0]])
    own_kv, both_qg = lax.optimization_barrier((own_kv, both_qg))
    across_kv = flipped(own_kv, "zh")
    core_kv = flipped(own_kv, "c")
    spread = jnp.broadcast_to(both_qg[None], (NX,) + both_qg.shape)
    all_qg = lax.all_to_all(spread, "x", 0, 0)
    far, live, across_kv = run_masks(key_tiles, across_kv)
    core_across_kv = flipped(across_kv, "c")
    work = work_lists.reshape(16, 64)
    kv = (own_kv, across_kv, core_kv, core_across_kv)

    stats = run_stats(live, all_qg, kv, far)
    stats = lax.all_to_all(stats, ("x", "p"), 0, 0)
    keep, send, dq = run_grads(live, work, all_qg, kv, far, stats)

    total = keep + flipped(send, "c").astype(jnp.float32)
    dkv_out = total[1].astype(jnp.bfloat16)
    from_across = flipped(dkv_out, "zh")
    dq_parts = lax.all_to_all(dq, "x", 0, 0)
    dq_sum = jnp.sum(dq_parts.astype(jnp.float32), axis=0).astype(jnp.bfloat16)
    dq_sum = lax.all_to_all(dq_sum.reshape(2, HALF, HD), "p", 0, 0)
    grad_queries = jnp.sum(dq_sum.astype(jnp.float32), axis=0).astype(jnp.bfloat16)
    grad_keys, grad_values = run_finish(total[0], from_across)
    return grad_queries[None, None], grad_keys[None, None], grad_values[None, None]


def solution(mesh):
    devices = mesh.devices.reshape(4, 2, 2, 16, 2)
    fine = Mesh(devices, ("x", "zh", "c", "n", "p"))
    spec = P(("x", "zh", "c"), ("n", "p"), None, None)
    return jax.shard_map(
        on_device,
        mesh=fine,
        in_specs=(spec, spec, spec, spec, P(), P()),
        out_specs=(spec, spec, spec),
        check_vma=False,
    )
```

```python
import functools

import jax
import jax.numpy as jnp
from jax import lax
from jax.experimental import pallas as pl
from jax.experimental.pallas import tpu as pltpu
from jax.sharding import Mesh, PartitionSpec as P

TILE = 128
HD = 128
HALF = 256
NX = 4
NCHUNK = 4
BLOCKS = 2 * NX
ROWS = BLOCKS * HALF
SCALE = HD**-0.5
SCALE2 = SCALE * 1.4426950408889634
FAR = 1e30


def dot_t(a, b):
    return lax.dot_general(a, b, (((1,), (1,)), ((), ())), preferred_element_type=jnp.float32)


def dot_n(a, b):
    return jnp.dot(a, b, preferred_element_type=jnp.float32)


def mask_kernel(tiles_ref, own_ref, across_ref, far_ref, live_ref, mine_ref, table_ref):
    mine_ref[0] = own_ref[...]
    mine_ref[1] = across_ref[...]
    x, zh, core, half = (lax.axis_index(name) for name in ("x", "zh", "c", "p"))
    tiles = tiles_ref[...]
    for k in range(2 * NCHUNK):
        chunk_zh = zh if k // 2 % 2 == 0 else 1 - zh
        chunk_core = core if k // 4 == 0 else 1 - core
        chunk_half = half if k // 2 % 2 == 0 else 1 - half
        key_id = (4 * x + 2 * chunk_zh + chunk_core) * 4 + 2 * chunk_half + k % 2
        hit = jnp.where(tiles == key_id, 0.0, FAR)
        table_ref[k] = jnp.broadcast_to(jnp.min(hit, axis=1, keepdims=True), (64, TILE))
    for n in range(NX):
        first = (4 * n + 2 * zh + core) * 4
        nearest = jnp.full((4, TILE), FAR, jnp.float32)
        for k in range(2 * NCHUNK):
            four = table_ref[k, pl.ds(first, 4), :]
            nearest = jnp.minimum(nearest, four)
            for h in range(2):
                far_ref[n, h, k : k + 1, :TILE] = four[2 * h : 2 * h + 1]
                far_ref[n, h, k : k + 1, TILE:] = four[2 * h + 1 : 2 * h + 2]
        live_ref[n] = (jnp.min(nearest) < 1.0).astype(jnp.int32)


def stats_kernel(live_ref, qg_ref, mine_ref, mate_ref, far_ref, out_ref):
    chunks = (mine_ref.at[0], mine_ref.at[1], mate_ref.at[0], mate_ref.at[1])

    def group(n, carry):
        @pl.when(live_ref[n] > 0)
        def _():
            for h in range(2):
                q = qg_ref[n, h, 0]
                g = qg_ref[n, h, 1]
                far = far_ref[n, h]
                scores = []
                top = jnp.full((1, HALF), -FAR, jnp.float32)
                for i, chunk in enumerate(chunks):
                    s = dot_t(chunk[0], q)
                    for t in range(2):
                        st = s[t * TILE : (t + 1) * TILE]
                        scores.append(st)
                        k = 2 * i + t
                        near = jnp.max(st, axis=0, keepdims=True) - far[k : k + 1]
                        top = jnp.maximum(top, near)
                top = top * SCALE2
                total = jnp.zeros((1, HALF), jnp.float32)
                weighted = jnp.zeros((1, HALF), jnp.float32)
                for i, chunk in enumerate(chunks):
                    gp = dot_t(chunk[1], g)
                    for t in range(2):
                        k = 2 * i + t
                        e = jnp.exp2(scores[k] * SCALE2 - (top + 4.0 * far[k : k + 1]))
                        total = total + jnp.sum(e, axis=0, keepdims=True)
                        weighted = weighted + jnp.sum(
                            e * gp[t * TILE : (t + 1) * TILE], axis=0, keepdims=True
                        )
                some = total > 0.0
                safe = jnp.where(some, total, 1.0)
                lse = jnp.where(some, top + jnp.log2(safe), -FAR)
                mean = jnp.where(some, weighted / safe, 0.0)
                for j in range(BLOCKS):
                    out_ref[j, n, h, :, :HALF] = lse
                    out_ref[j, n, h, :, HALF:] = mean

        @pl.when(live_ref[n] == 0)
        def _():
            for j in range(BLOCKS):
                for h in range(2):
                    out_ref[j, n, h, :, :HALF] = jnp.full((1, HALF), -FAR, jnp.float32)
                    out_ref[j, n, h, :, HALF:] = jnp.zeros((1, HALF), jnp.float32)

        return carry

    lax.fori_loop(0, NX, group, 0)


def grads_kernel(
    live_ref,
    work_ref,
    qg_ref,
    mine_ref,
    mate_ref,
    far_ref,
    stats_ref,
    keep_ref,
    send_ref,
    dq_ref,
    dk_acc,
    dv_acc,
    kt_ref,
    ds_ref,
):
    zh, core, head = (lax.axis_index(name) for name in ("zh", "c", "n"))
    chunks = (mine_ref.at[0], mine_ref.at[1], mate_ref.at[0], mate_ref.at[1])
    dk_acc[...] = jnp.zeros_like(dk_acc)
    dv_acc[...] = jnp.zeros_like(dv_acc)
    for i, chunk in enumerate(chunks):
        kt_ref[:, i * HALF : (i + 1) * HALF] = chunk[0].T

    def group(n, carry):
        @pl.when(live_ref[n] > 0)
        def _():
            q_all = qg_ref[n, :, 0].reshape(2 * HALF, HD)
            g_all = qg_ref[n, :, 1].reshape(2 * HALF, HD)
            rows_stats = []
            for h in range(2):
                lse_parts = [stats_ref[j, n, h, :, :HALF] for j in range(BLOCKS)]
                top = functools.reduce(jnp.maximum, lse_parts)
                total = jnp.zeros((1, HALF), jnp.float32)
                weighted = jnp.zeros((1, HALF), jnp.float32)
                for j in range(BLOCKS):
                    w = jnp.exp2(lse_parts[j] - top)
                    total = total + w
                    weighted = weighted + w * stats_ref[j, n, h, :, HALF:]
                rows_stats.append((top + jnp.log2(total), weighted / total))
            for i, chunk in enumerate(chunks):
                rows = slice(i * HALF, (i + 1) * HALF)
                ps, ds = [], []
                for h in range(2):
                    lse, delta = rows_stats[h]
                    s = dot_t(chunk[0], qg_ref[n, h, 0])
                    gp = dot_t(chunk[1], qg_ref[n, h, 1])
                    p_parts, d_parts = [], []
                    for t in range(2):
                        k = 2 * i + t
                        part = slice(t * TILE, (t + 1) * TILE)
                        shift = lse + 4.0 * far_ref[n, h, k : k + 1, :]
                        p = jnp.exp2(s[part] * SCALE2 - shift)
                        p_parts.append(p.astype(jnp.bfloat16))
                        d_parts.append((p * (gp[part] - delta)).astype(jnp.bfloat16))
                    ps.append(jnp.concatenate(p_parts, axis=0))
                    d = jnp.concatenate(d_parts, axis=0)
                    ds.append(d)
                    ds_ref[h, rows] = d
                dv_acc[rows] += dot_n(jnp.concatenate(ps, axis=1), g_all)
                dk_acc[rows] += dot_n(jnp.concatenate(ds, axis=1), q_all)
            for h in range(2):
                dq = (dot_n(kt_ref[...], ds_ref[h]) * SCALE).T.astype(jnp.bfloat16)
                for t in range(2):
                    slot = jnp.int32(3)
                    for w in range(3):
                        listed = work_ref[4 * n + 2 * zh + core, 4 * head + w]
                        slot = jnp.where(listed == 2 * h + t, w, slot)
                    dq_ref[n, slot] = dq[t * TILE : (t + 1) * TILE]

        @pl.when(live_ref[n] == 0)
        def _():
            dq_ref[n] = jnp.zeros((4, TILE, HD), jnp.bfloat16)

        return carry

    lax.fori_loop(0, NX, group, 0)
    for i in range(2):
        rows = slice(i * HALF, (i + 1) * HALF)
        keep_ref[i, 0] = dk_acc[rows] * SCALE
        keep_ref[i, 1] = dv_acc[rows]
        rows = slice((i + 2) * HALF, (i + 3) * HALF)
        send_ref[i, 0] = (dk_acc[rows] * SCALE).astype(jnp.bfloat16)
        send_ref[i, 1] = dv_acc[rows].astype(jnp.bfloat16)


VMEM = pl.BlockSpec(memory_space=pltpu.VMEM)
SMEM = pl.BlockSpec(memory_space=pltpu.SMEM)


def flipped(value, axis):
    return lax.ppermute(value, axis, [(0, 1), (1, 0)])


def across(value):
    return lax.ppermute(value, ("zh", "p"), [(0, 3), (1, 2), (2, 1), (3, 0)])


def run_masks(tiles, own, arrived):
    return pl.pallas_call(
        mask_kernel,
        out_shape=[
            jax.ShapeDtypeStruct((NX, 2, 2 * NCHUNK, HALF), jnp.float32),
            jax.ShapeDtypeStruct((NX,), jnp.int32),
            jax.ShapeDtypeStruct((2,) + own.shape, own.dtype),
        ],
        in_specs=[VMEM] * 3,
        out_specs=[VMEM, SMEM, VMEM],
        scratch_shapes=[pltpu.VMEM((2 * NCHUNK, 64, TILE), jnp.float32)],
        compiler_params=pltpu.CompilerParams(vmem_limit_bytes=8 * 1024 * 1024),
        cost_estimate=pl.CostEstimate(flops=10**11, bytes_accessed=2**20, transcendentals=0),
        name="masks",
    )(tiles, own, arrived)


def run_stats(live, qg, kv, far):
    return pl.pallas_call(
        stats_kernel,
        out_shape=jax.ShapeDtypeStruct((BLOCKS, NX, 2, 1, 2 * HALF), jnp.float32),
        in_specs=[SMEM] + [VMEM] * 4,
        out_specs=VMEM,
        compiler_params=pltpu.CompilerParams(vmem_limit_bytes=32 * 1024 * 1024),
        cost_estimate=pl.CostEstimate(flops=10**9, bytes_accessed=2**21, transcendentals=2**21),
        name="stats",
    )(live, qg, *kv, far)


def run_grads(live, work, qg, kv, far, stats):
    return pl.pallas_call(
        grads_kernel,
        out_shape=[
            jax.ShapeDtypeStruct((2, 2, HALF, HD), jnp.float32),
            jax.ShapeDtypeStruct((2, 2, HALF, HD), jnp.bfloat16),
            jax.ShapeDtypeStruct((NX, 4, TILE, HD), jnp.bfloat16),
        ],
        in_specs=[SMEM, SMEM] + [VMEM] * 5,
        out_specs=[VMEM] * 3,
        scratch_shapes=[
            pltpu.VMEM((NCHUNK * HALF, HD), jnp.float32),
            pltpu.VMEM((NCHUNK * HALF, HD), jnp.float32),
            pltpu.VMEM((HD, NCHUNK * HALF), jnp.bfloat16),
            pltpu.VMEM((2, NCHUNK * HALF, HALF), jnp.bfloat16),
        ],
        compiler_params=pltpu.CompilerParams(vmem_limit_bytes=24 * 1024 * 1024),
        cost_estimate=pl.CostEstimate(flops=2 * 10**9, bytes_accessed=2**21, transcendentals=2**21),
        name="grads",
    )(live, work, qg, *kv, far, stats)


def finish_kernel(total_ref, arrived_ref, dk_ref, dv_ref):
    dk_ref[...] = (total_ref[0, 0] + arrived_ref[0].astype(jnp.float32)).astype(jnp.bfloat16)
    dv_ref[...] = (total_ref[0, 1] + arrived_ref[1].astype(jnp.float32)).astype(jnp.bfloat16)


def run_finish(total, arrived):
    return pl.pallas_call(
        finish_kernel,
        out_shape=[jax.ShapeDtypeStruct((HALF, HD), jnp.bfloat16)] * 2,
        in_specs=[VMEM] * 2,
        out_specs=[VMEM] * 2,
        compiler_params=pltpu.CompilerParams(vmem_limit_bytes=8 * 1024 * 1024),
        cost_estimate=pl.CostEstimate(flops=10**11, bytes_accessed=2**20, transcendentals=0),
        name="finish",
    )(total, arrived)


def sum_kernel(parts_ref, dq_ref):
    dq = parts_ref[0].astype(jnp.float32)
    for j in range(1, BLOCKS):
        dq = dq + parts_ref[j].astype(jnp.float32)
    dq_ref[...] = dq.astype(jnp.bfloat16)


def run_sum(parts):
    return pl.pallas_call(
        sum_kernel,
        out_shape=jax.ShapeDtypeStruct((HALF, HD), jnp.bfloat16),
        in_specs=[VMEM],
        out_specs=VMEM,
        compiler_params=pltpu.CompilerParams(vmem_limit_bytes=8 * 1024 * 1024),
        name="sum",
    )(parts)


def on_device(queries, keys, values, grad_out, key_tiles, work_lists):
    own_qg = jnp.stack([queries[0, 0], grad_out[0, 0]])
    both_qg = lax.all_gather(own_qg, "p")
    own_kv = jnp.stack([keys[0, 0], values[0, 0]])
    own_kv, both_qg = lax.optimization_barrier((own_kv, both_qg))
    across_kv = across(own_kv)
    spread = jnp.broadcast_to(both_qg[None], (NX,) + both_qg.shape)
    all_qg = lax.all_to_all(spread, "x", 0, 0)
    far, live, mine = run_masks(key_tiles, own_kv, across_kv)
    kv = (mine, flipped(mine, "c"))
    work = work_lists.reshape(16, 64)

    stats = run_stats(live, all_qg, kv, far)
    stats = lax.all_to_all(stats, ("x", "p"), 0, 0)
    keep, send, dq = run_grads(live, work, all_qg, kv, far, stats)

    total = keep + flipped(send, "c").astype(jnp.float32)
    dkv_out = total[1].astype(jnp.bfloat16)
    dkv_out, dq = lax.optimization_barrier((dkv_out, dq))
    from_across = across(dkv_out)
    dq = dq.reshape(BLOCKS, HALF, HD)
    dq_parts = lax.all_to_all(dq, ("x", "p"), 0, 0)
    grad_keys, grad_values = run_finish(total, from_across)
    outs = (run_sum(dq_parts), grad_keys, grad_values)
    return tuple(out[None, None] for out in outs)


def solution(mesh):
    devices = mesh.devices.reshape(4, 2, 2, 16, 2)
    fine = Mesh(devices, ("x", "zh", "c", "n", "p"))
    spec = P(("x", "zh", "c"), ("n", "p"), None, None)
    return jax.shard_map(
        on_device,
        mesh=fine,
        in_specs=(spec, spec, spec, spec, P(), P()),
        out_specs=(spec, spec, spec),
        check_vma=False,
    )
```

```python
import functools

import jax
import jax.numpy as jnp
from jax import lax
from jax.experimental import pallas as pl
from jax.experimental.pallas import tpu as pltpu
from jax.sharding import Mesh, PartitionSpec as P

TILE = 128
HD = 128
HALF = 256
NX = 4
NCHUNK = 4
BLOCKS = 2 * NX
ROWS = BLOCKS * HALF
SCALE = HD**-0.5
SCALE2 = SCALE * 1.4426950408889634
FAR = 1e30


def dot_t(a, b):
    return lax.dot_general(a, b, (((1,), (1,)), ((), ())), preferred_element_type=jnp.float32)


def dot_n(a, b):
    return jnp.dot(a, b, preferred_element_type=jnp.float32)


def spread_kernel(own_ref, mate_ref, out_ref):
    half = lax.axis_index("p")
    for j in range(NX):
        out_ref[j, half] = own_ref[...]
        out_ref[j, 1 - half] = mate_ref[...]


def mask_kernel(tiles_ref, own_ref, across_ref, far_ref, live_ref, mine_ref, table_ref):
    mine_ref[0] = own_ref[...]
    mine_ref[1] = across_ref[...]
    x, zh, core, half = (lax.axis_index(name) for name in ("x", "zh", "c", "p"))
    tiles = tiles_ref[...]
    for k in range(2 * NCHUNK):
        chunk_zh = zh if k // 2 % 2 == 0 else 1 - zh
        chunk_core = core if k // 4 == 0 else 1 - core
        chunk_half = half if k // 2 % 2 == 0 else 1 - half
        key_id = (4 * x + 2 * chunk_zh + chunk_core) * 4 + 2 * chunk_half + k % 2
        hit = jnp.where(tiles == key_id, 0.0, FAR)
        table_ref[k] = jnp.broadcast_to(jnp.min(hit, axis=1, keepdims=True), (64, TILE))
    for n in range(NX):
        first = (4 * n + 2 * zh + core) * 4
        nearest = jnp.full((4, TILE), FAR, jnp.float32)
        for k in range(2 * NCHUNK):
            four = table_ref[k, pl.ds(first, 4), :]
            nearest = jnp.minimum(nearest, four)
            for h in range(2):
                far_ref[n, h, k : k + 1, :TILE] = four[2 * h : 2 * h + 1]
                far_ref[n, h, k : k + 1, TILE:] = four[2 * h + 1 : 2 * h + 2]
        live_ref[n] = (jnp.min(nearest) < 1.0).astype(jnp.int32)


def stats_kernel(live_ref, qg_ref, mine_ref, mate_ref, far_ref, out_ref):
    chunks = (mine_ref.at[0], mine_ref.at[1], mate_ref.at[0], mate_ref.at[1])

    def group(n, carry):
        @pl.when(live_ref[n] > 0)
        def _():
            for h in range(2):
                q = qg_ref[n, h, 0]
                g = qg_ref[n, h, 1]
                far = far_ref[n, h]
                scores = []
                top = jnp.full((1, HALF), -FAR, jnp.float32)
                for i, chunk in enumerate(chunks):
                    s = dot_t(chunk[0], q)
                    for t in range(2):
                        st = s[t * TILE : (t + 1) * TILE]
                        scores.append(st)
                        k = 2 * i + t
                        near = jnp.max(st, axis=0, keepdims=True) - far[k : k + 1]
                        top = jnp.maximum(top, near)
                top = top * SCALE2
                total = jnp.zeros((1, HALF), jnp.float32)
                weighted = jnp.zeros((1, HALF), jnp.float32)
                for i, chunk in enumerate(chunks):
                    gp = dot_t(chunk[1], g)
                    for t in range(2):
                        k = 2 * i + t
                        e = jnp.exp2(scores[k] * SCALE2 - (top + 4.0 * far[k : k + 1]))
                        total = total + jnp.sum(e, axis=0, keepdims=True)
                        weighted = weighted + jnp.sum(
                            e * gp[t * TILE : (t + 1) * TILE], axis=0, keepdims=True
                        )
                some = total > 0.0
                safe = jnp.where(some, total, 1.0)
                lse = jnp.where(some, top + jnp.log2(safe), -FAR)
                mean = jnp.where(some, weighted / safe, 0.0)
                for j in range(BLOCKS):
                    out_ref[j, n, h, :, :HALF] = lse
                    out_ref[j, n, h, :, HALF:] = mean

        @pl.when(live_ref[n] == 0)
        def _():
            for j in range(BLOCKS):
                for h in range(2):
                    out_ref[j, n, h, :, :HALF] = jnp.full((1, HALF), -FAR, jnp.float32)
                    out_ref[j, n, h, :, HALF:] = jnp.zeros((1, HALF), jnp.float32)

        return carry

    lax.fori_loop(0, NX, group, 0)


def grads_kernel(
    live_ref,
    work_ref,
    qg_ref,
    mine_ref,
    mate_ref,
    far_ref,
    stats_ref,
    keep_ref,
    send_ref,
    dq_ref,
    dk_acc,
    dv_acc,
    kt_ref,
    ds_ref,
):
    zh, core, head = (lax.axis_index(name) for name in ("zh", "c", "n"))
    chunks = (mine_ref.at[0], mine_ref.at[1], mate_ref.at[0], mate_ref.at[1])
    dk_acc[...] = jnp.zeros_like(dk_acc)
    dv_acc[...] = jnp.zeros_like(dv_acc)
    for i, chunk in enumerate(chunks):
        kt_ref[:, i * HALF : (i + 1) * HALF] = chunk[0].T

    def group(n, carry):
        @pl.when(live_ref[n] > 0)
        def _():
            q_all = qg_ref[n, :, 0].reshape(2 * HALF, HD)
            g_all = qg_ref[n, :, 1].reshape(2 * HALF, HD)
            rows_stats = []
            for h in range(2):
                lse_parts = [stats_ref[j, n, h, :, :HALF] for j in range(BLOCKS)]
                top = functools.reduce(jnp.maximum, lse_parts)
                total = jnp.zeros((1, HALF), jnp.float32)
                weighted = jnp.zeros((1, HALF), jnp.float32)
                for j in range(BLOCKS):
                    w = jnp.exp2(lse_parts[j] - top)
                    total = total + w
                    weighted = weighted + w * stats_ref[j, n, h, :, HALF:]
                rows_stats.append((top + jnp.log2(total), weighted / total))
            for i, chunk in enumerate(chunks):
                rows = slice(i * HALF, (i + 1) * HALF)
                ps, ds = [], []
                for h in range(2):
                    lse, delta = rows_stats[h]
                    s = dot_t(chunk[0], qg_ref[n, h, 0])
                    gp = dot_t(chunk[1], qg_ref[n, h, 1])
                    p_parts, d_parts = [], []
                    for t in range(2):
                        k = 2 * i + t
                        part = slice(t * TILE, (t + 1) * TILE)
                        shift = lse + 4.0 * far_ref[n, h, k : k + 1, :]
                        p = jnp.exp2(s[part] * SCALE2 - shift)
                        p_parts.append(p.astype(jnp.bfloat16))
                        d_parts.append((p * (gp[part] - delta)).astype(jnp.bfloat16))
                    ps.append(jnp.concatenate(p_parts, axis=0))
                    d = jnp.concatenate(d_parts, axis=0)
                    ds.append(d)
                    ds_ref[h, rows] = d
                dv_acc[rows] += dot_n(jnp.concatenate(ps, axis=1), g_all)
                dk_acc[rows] += dot_n(jnp.concatenate(ds, axis=1), q_all)
            for h in range(2):
                dq = (dot_n(kt_ref[...], ds_ref[h]) * SCALE).T.astype(jnp.bfloat16)
                for t in range(2):
                    slot = jnp.int32(3)
                    for w in range(3):
                        listed = work_ref[4 * n + 2 * zh + core, 4 * head + w]
                        slot = jnp.where(listed == 2 * h + t, w, slot)
                    dq_ref[n, slot] = dq[t * TILE : (t + 1) * TILE]

        @pl.when(live_ref[n] == 0)
        def _():
            dq_ref[n] = jnp.zeros((4, TILE, HD), jnp.bfloat16)

        return carry

    lax.fori_loop(0, NX, group, 0)
    for i in range(2):
        rows = slice(i * HALF, (i + 1) * HALF)
        keep_ref[i, 0] = dk_acc[rows] * SCALE
        keep_ref[i, 1] = dv_acc[rows]
        rows = slice((i + 2) * HALF, (i + 3) * HALF)
        send_ref[i, 0] = (dk_acc[rows] * SCALE).astype(jnp.bfloat16)
        send_ref[i, 1] = dv_acc[rows].astype(jnp.bfloat16)


VMEM = pl.BlockSpec(memory_space=pltpu.VMEM)
SMEM = pl.BlockSpec(memory_space=pltpu.SMEM)


def flipped(value, axis):
    return lax.ppermute(value, axis, [(0, 1), (1, 0)])


def across(value):
    return lax.ppermute(value, ("zh", "p"), [(0, 3), (1, 2), (2, 1), (3, 0)])


def run_spread(own, mate):
    return pl.pallas_call(
        spread_kernel,
        out_shape=jax.ShapeDtypeStruct((NX, 2) + own.shape, own.dtype),
        in_specs=[VMEM] * 2,
        out_specs=VMEM,
        compiler_params=pltpu.CompilerParams(vmem_limit_bytes=8 * 1024 * 1024),
        name="spread",
    )(own, mate)


def run_masks(tiles, own, arrived):
    return pl.pallas_call(
        mask_kernel,
        out_shape=[
            jax.ShapeDtypeStruct((NX, 2, 2 * NCHUNK, HALF), jnp.float32),
            jax.ShapeDtypeStruct((NX,), jnp.int32),
            jax.ShapeDtypeStruct((2,) + own.shape, own.dtype),
        ],
        in_specs=[VMEM] * 3,
        out_specs=[VMEM, SMEM, VMEM],
        scratch_shapes=[pltpu.VMEM((2 * NCHUNK, 64, TILE), jnp.float32)],
        compiler_params=pltpu.CompilerParams(vmem_limit_bytes=8 * 1024 * 1024),
        cost_estimate=pl.CostEstimate(flops=10**11, bytes_accessed=2**20, transcendentals=0),
        name="masks",
    )(tiles, own, arrived)


def run_stats(live, qg, kv, far):
    return pl.pallas_call(
        stats_kernel,
        out_shape=jax.ShapeDtypeStruct((BLOCKS, NX, 2, 1, 2 * HALF), jnp.float32),
        in_specs=[SMEM] + [VMEM] * 4,
        out_specs=VMEM,
        compiler_params=pltpu.CompilerParams(vmem_limit_bytes=32 * 1024 * 1024),
        cost_estimate=pl.CostEstimate(flops=10**9, bytes_accessed=2**21, transcendentals=2**21),
        name="stats",
    )(live, qg, *kv, far)


def run_grads(live, work, qg, kv, far, stats):
    return pl.pallas_call(
        grads_kernel,
        out_shape=[
            jax.ShapeDtypeStruct((2, 2, HALF, HD), jnp.float32),
            jax.ShapeDtypeStruct((2, 2, HALF, HD), jnp.bfloat16),
            jax.ShapeDtypeStruct((NX, 4, TILE, HD), jnp.bfloat16),
        ],
        in_specs=[SMEM, SMEM] + [VMEM] * 5,
        out_specs=[VMEM] * 3,
        scratch_shapes=[
            pltpu.VMEM((NCHUNK * HALF, HD), jnp.float32),
            pltpu.VMEM((NCHUNK * HALF, HD), jnp.float32),
            pltpu.VMEM((HD, NCHUNK * HALF), jnp.bfloat16),
            pltpu.VMEM((2, NCHUNK * HALF, HALF), jnp.bfloat16),
        ],
        compiler_params=pltpu.CompilerParams(vmem_limit_bytes=24 * 1024 * 1024),
        cost_estimate=pl.CostEstimate(flops=2 * 10**9, bytes_accessed=2**21, transcendentals=2**21),
        name="grads",
    )(live, work, qg, *kv, far, stats)


def finish_kernel(total_ref, arrived_ref, dk_ref, dv_ref):
    dk_ref[...] = (total_ref[0, 0] + arrived_ref[0].astype(jnp.float32)).astype(jnp.bfloat16)
    dv_ref[...] = (total_ref[0, 1] + arrived_ref[1].astype(jnp.float32)).astype(jnp.bfloat16)


def run_finish(total, arrived):
    return pl.pallas_call(
        finish_kernel,
        out_shape=[jax.ShapeDtypeStruct((HALF, HD), jnp.bfloat16)] * 2,
        in_specs=[VMEM] * 2,
        out_specs=[VMEM] * 2,
        compiler_params=pltpu.CompilerParams(vmem_limit_bytes=8 * 1024 * 1024),
        cost_estimate=pl.CostEstimate(flops=10**11, bytes_accessed=2**20, transcendentals=0),
        name="finish",
    )(total, arrived)


def sum_kernel(parts_ref, dq_ref):
    dq = parts_ref[0].astype(jnp.float32)
    for j in range(1, BLOCKS):
        dq = dq + parts_ref[j].astype(jnp.float32)
    dq_ref[...] = dq.astype(jnp.bfloat16)


def run_sum(parts):
    return pl.pallas_call(
        sum_kernel,
        out_shape=jax.ShapeDtypeStruct((HALF, HD), jnp.bfloat16),
        in_specs=[VMEM],
        out_specs=VMEM,
        compiler_params=pltpu.CompilerParams(vmem_limit_bytes=8 * 1024 * 1024),
        name="sum",
    )(parts)


def on_device(queries, keys, values, grad_out, key_tiles, work_lists):
    own_qg = jnp.stack([queries[0, 0], grad_out[0, 0]])
    mate_qg = flipped(own_qg, "p")
    own_kv = jnp.stack([keys[0, 0], values[0, 0]])
    across_kv = across(own_kv)
    spread = run_spread(own_qg, mate_qg)
    all_qg = lax.all_to_all(spread, "x", 0, 0)
    far, live, mine = run_masks(key_tiles, own_kv, across_kv)
    kv = (mine, flipped(mine, "c"))
    work = work_lists.reshape(16, 64)

    stats = run_stats(live, all_qg, kv, far)
    stats = lax.all_to_all(stats, ("x", "p"), 0, 0)
    keep, send, dq = run_grads(live, work, all_qg, kv, far, stats)

    total = keep + flipped(send, "c").astype(jnp.float32)
    dkv_out = total[1].astype(jnp.bfloat16)
    dkv_out, dq = lax.optimization_barrier((dkv_out, dq))
    from_across = across(dkv_out)
    dq = dq.reshape(BLOCKS, HALF, HD)
    dq_parts = lax.all_to_all(dq, ("x", "p"), 0, 0)
    grad_keys, grad_values = run_finish(total, from_across)
    outs = (run_sum(dq_parts), grad_keys, grad_values)
    return tuple(out[None, None] for out in outs)


def solution(mesh):
    devices = mesh.devices.reshape(4, 2, 2, 16, 2)
    fine = Mesh(devices, ("x", "zh", "c", "n", "p"))
    spec = P(("x", "zh", "c"), ("n", "p"), None, None)
    return jax.shard_map(
        on_device,
        mesh=fine,
        in_specs=(spec, spec, spec, spec, P(), P()),
        out_specs=(spec, spec, spec),
        check_vma=False,
    )
```

```python
import functools

import jax
import jax.numpy as jnp
from jax import lax
from jax.experimental import pallas as pl
from jax.experimental.pallas import tpu as pltpu
from jax.sharding import Mesh, PartitionSpec as P

TILE = 128
HD = 128
HALF = 256
NX = 4
NCHUNK = 4
BLOCKS = 2 * NX
ROWS = BLOCKS * HALF
SCALE = HD**-0.5
SCALE2 = SCALE * 1.4426950408889634
FAR = 1e30


def dot_t(a, b):
    return lax.dot_general(a, b, (((1,), (1,)), ((), ())), preferred_element_type=jnp.float32)


def dot_n(a, b):
    return jnp.dot(a, b, preferred_element_type=jnp.float32)


def spread_kernel(own_ref, mate_ref, out_ref):
    half = lax.axis_index("p")
    for j in range(NX):
        out_ref[j, half] = own_ref[...]
        out_ref[j, 1 - half] = mate_ref[...]


def mask_kernel(tiles_ref, after_ref, far_ref, live_ref, table_ref):
    x, zh, core, half = (lax.axis_index(name) for name in ("x", "zh", "c", "p"))
    tiles = tiles_ref[...]
    for k in range(2 * NCHUNK):
        chunk_zh = zh if k // 4 == 0 else 1 - zh
        chunk_half = half if k // 4 == 0 else 1 - half
        key_id = (4 * x + 2 * chunk_zh + k // 2 % 2) * 4 + 2 * chunk_half + k % 2
        hit = jnp.where(tiles == key_id, 0.0, FAR)
        table_ref[k] = jnp.broadcast_to(jnp.min(hit, axis=1, keepdims=True), (64, TILE))
    for n in range(NX):
        first = (4 * n + 2 * zh + core) * 4
        for side in range(2):
            nearest = jnp.full((4, TILE), FAR, jnp.float32)
            for k in range(NCHUNK * side, NCHUNK * (side + 1)):
                four = table_ref[k, pl.ds(first, 4), :]
                nearest = jnp.minimum(nearest, four)
                for h in range(2):
                    far_ref[n, h, k : k + 1, :TILE] = four[2 * h : 2 * h + 1]
                    far_ref[n, h, k : k + 1, TILE:] = four[2 * h + 1 : 2 * h + 2]
            live_ref[2 * n + side] = (jnp.min(nearest) < 1.0).astype(jnp.int32)


def by_sides(live_ref, n, work, nothing):
    here, there = live_ref[2 * n], live_ref[2 * n + 1]
    pl.when((here > 0) & (there > 0))(lambda: work((0, 1, 2, 3)))
    pl.when((here > 0) & (there == 0))(lambda: work((0, 1)))
    pl.when((here == 0) & (there > 0))(lambda: work((2, 3)))
    pl.when((here == 0) & (there == 0))(nothing)


def stats_kernel(live_ref, qg_ref, here_ref, there_ref, far_ref, out_ref):
    chunks = (here_ref.at[0], here_ref.at[1], there_ref.at[0], there_ref.at[1])

    def group(n, carry):
        def work(subset):
            for h in range(2):
                q = qg_ref[n, h, 0]
                g = qg_ref[n, h, 1]
                far = far_ref[n, h]
                scores = {}
                top = jnp.full((1, HALF), -FAR, jnp.float32)
                for i in subset:
                    s = dot_t(chunks[i][0], q)
                    for t in range(2):
                        k = 2 * i + t
                        scores[k] = s[t * TILE : (t + 1) * TILE]
                        near = jnp.max(scores[k], axis=0, keepdims=True) - far[k : k + 1]
                        top = jnp.maximum(top, near)
                top = top * SCALE2
                total = jnp.zeros((1, HALF), jnp.float32)
                weighted = jnp.zeros((1, HALF), jnp.float32)
                for i in subset:
                    gp = dot_t(chunks[i][1], g)
                    for t in range(2):
                        k = 2 * i + t
                        e = jnp.exp2(scores[k] * SCALE2 - (top + 4.0 * far[k : k + 1]))
                        total = total + jnp.sum(e, axis=0, keepdims=True)
                        weighted = weighted + jnp.sum(
                            e * gp[t * TILE : (t + 1) * TILE], axis=0, keepdims=True
                        )
                some = total > 0.0
                safe = jnp.where(some, total, 1.0)
                lse = jnp.where(some, top + jnp.log2(safe), -FAR)
                mean = jnp.where(some, weighted / safe, 0.0)
                for j in range(BLOCKS):
                    out_ref[j, n, h, :, :HALF] = lse
                    out_ref[j, n, h, :, HALF:] = mean

        def nothing():
            for j in range(BLOCKS):
                for h in range(2):
                    out_ref[j, n, h, :, :HALF] = jnp.full((1, HALF), -FAR, jnp.float32)
                    out_ref[j, n, h, :, HALF:] = jnp.zeros((1, HALF), jnp.float32)

        by_sides(live_ref, n, work, nothing)
        return carry

    lax.fori_loop(0, NX, group, 0)


def grads_kernel(
    live_ref,
    work_ref,
    qg_ref,
    here_ref,
    there_ref,
    far_ref,
    stats_ref,
    keep_ref,
    send_ref,
    dq_ref,
    dk_acc,
    dv_acc,
    kt_ref,
    ds_ref,
    dq_buf,
    sems,
):
    zh, core, head = (lax.axis_index(name) for name in ("zh", "c", "n"))
    chunks = (here_ref.at[0], here_ref.at[1], there_ref.at[0], there_ref.at[1])
    dk_acc[...] = jnp.zeros_like(dk_acc)
    dv_acc[...] = jnp.zeros_like(dv_acc)
    for i, chunk in enumerate(chunks):
        kt_ref[:, i * HALF : (i + 1) * HALF] = chunk[0].T

    def group(n, carry):
        def work(subset):
            q_all = qg_ref[n, :, 0].reshape(2 * HALF, HD)
            g_all = qg_ref[n, :, 1].reshape(2 * HALF, HD)
            rows_stats = []
            for h in range(2):
                lse_parts = [stats_ref[j, n, h, :, :HALF] for j in range(BLOCKS)]
                top = functools.reduce(jnp.maximum, lse_parts)
                total = jnp.zeros((1, HALF), jnp.float32)
                weighted = jnp.zeros((1, HALF), jnp.float32)
                for j in range(BLOCKS):
                    w = jnp.exp2(lse_parts[j] - top)
                    total = total + w
                    weighted = weighted + w * stats_ref[j, n, h, :, HALF:]
                rows_stats.append((top + jnp.log2(total), weighted / total))
            for i in subset:
                rows = slice(i * HALF, (i + 1) * HALF)
                ps, ds = [], []
                for h in range(2):
                    lse, delta = rows_stats[h]
                    s = dot_t(chunks[i][0], qg_ref[n, h, 0])
                    gp = dot_t(chunks[i][1], qg_ref[n, h, 1])
                    p_parts, d_parts = [], []
                    for t in range(2):
                        k = 2 * i + t
                        part = slice(t * TILE, (t + 1) * TILE)
                        shift = lse + 4.0 * far_ref[n, h, k : k + 1, :]
                        p = jnp.exp2(s[part] * SCALE2 - shift)
                        p_parts.append(p.astype(jnp.bfloat16))
                        d_parts.append((p * (gp[part] - delta)).astype(jnp.bfloat16))
                    ps.append(jnp.concatenate(p_parts, axis=0))
                    d = jnp.concatenate(d_parts, axis=0)
                    ds.append(d)
                    ds_ref[h, rows] = d
                dv_acc[rows] += dot_n(jnp.concatenate(ps, axis=1), g_all)
                dk_acc[rows] += dot_n(jnp.concatenate(ds, axis=1), q_all)
            used = slice(subset[0] * HALF, (subset[-1] + 1) * HALF)
            for h in range(2):
                dq = (dot_n(kt_ref[:, used], ds_ref[h, used]) * SCALE).T.astype(jnp.bfloat16)
                for t in range(2):
                    slot = jnp.int32(3)
                    for w in range(3):
                        listed = work_ref[4 * n + 2 * zh + core, 4 * head + w]
                        slot = jnp.where(listed == 2 * h + t, w, slot)
                    dq_buf[n, slot] = dq[t * TILE : (t + 1) * TILE]

        def nothing():
            dq_buf[n] = jnp.zeros((4, TILE, HD), jnp.bfloat16)

        by_sides(live_ref, n, work, nothing)
        pltpu.make_async_copy(dq_buf.at[n], dq_ref.at[n], sems.at[n]).start()
        return carry

    lax.fori_loop(0, NX, group, 0)
    for i in range(2):
        rows = pl.ds((2 * i + core) * HALF, HALF)
        keep_ref[i, 0] = dk_acc[rows] * SCALE
        keep_ref[i, 1] = dv_acc[rows]
        rows = pl.ds((2 * i + 1 - core) * HALF, HALF)
        send_ref[i, 0] = (dk_acc[rows] * SCALE).astype(jnp.bfloat16)
        send_ref[i, 1] = dv_acc[rows].astype(jnp.bfloat16)
    for n in range(NX):
        pltpu.make_async_copy(dq_buf.at[n], dq_ref.at[n], sems.at[n]).wait()


VMEM = pl.BlockSpec(memory_space=pltpu.VMEM)
SMEM = pl.BlockSpec(memory_space=pltpu.SMEM)


def flipped(value, axis):
    return lax.ppermute(value, axis, [(0, 1), (1, 0)])


def across(value):
    return lax.ppermute(value, ("zh", "p"), [(0, 3), (1, 2), (2, 1), (3, 0)])


def run_spread(own, mate):
    return pl.pallas_call(
        spread_kernel,
        out_shape=jax.ShapeDtypeStruct((NX, 2) + own.shape, own.dtype),
        in_specs=[VMEM] * 2,
        out_specs=VMEM,
        compiler_params=pltpu.CompilerParams(vmem_limit_bytes=8 * 1024 * 1024),
        name="spread",
    )(own, mate)


def run_masks(tiles, after):
    return pl.pallas_call(
        mask_kernel,
        out_shape=[
            jax.ShapeDtypeStruct((NX, 2, 2 * NCHUNK, HALF), jnp.float32),
            jax.ShapeDtypeStruct((2 * NX,), jnp.int32),
        ],
        in_specs=[VMEM, pl.BlockSpec(memory_space=pl.ANY)],
        out_specs=[VMEM, SMEM],
        scratch_shapes=[pltpu.VMEM((2 * NCHUNK, 64, TILE), jnp.float32)],
        compiler_params=pltpu.CompilerParams(vmem_limit_bytes=8 * 1024 * 1024),
        cost_estimate=pl.CostEstimate(flops=10**10, bytes_accessed=2**20, transcendentals=0),
        name="masks",
    )(tiles, after)


def run_stats(live, qg, kv, far):
    return pl.pallas_call(
        stats_kernel,
        out_shape=jax.ShapeDtypeStruct((BLOCKS, NX, 2, 1, 2 * HALF), jnp.float32),
        in_specs=[SMEM] + [VMEM] * 4,
        out_specs=VMEM,
        compiler_params=pltpu.CompilerParams(vmem_limit_bytes=32 * 1024 * 1024),
        cost_estimate=pl.CostEstimate(flops=10**9, bytes_accessed=2**21, transcendentals=2**21),
        name="stats",
    )(live, qg, *kv, far)


def run_grads(live, work, qg, kv, far, stats):
    return pl.pallas_call(
        grads_kernel,
        out_shape=[
            jax.ShapeDtypeStruct((2, 2, HALF, HD), jnp.float32),
            jax.ShapeDtypeStruct((2, 2, HALF, HD), jnp.bfloat16),
            jax.ShapeDtypeStruct((NX, 4, TILE, HD), jnp.bfloat16),
        ],
        in_specs=[SMEM, SMEM] + [VMEM] * 5,
        out_specs=[VMEM, VMEM, pl.BlockSpec(memory_space=pl.ANY)],
        scratch_shapes=[
            pltpu.VMEM((NCHUNK * HALF, HD), jnp.float32),
            pltpu.VMEM((NCHUNK * HALF, HD), jnp.float32),
            pltpu.VMEM((HD, NCHUNK * HALF), jnp.bfloat16),
            pltpu.VMEM((2, NCHUNK * HALF, HALF), jnp.bfloat16),
            pltpu.VMEM((NX, 4, TILE, HD), jnp.bfloat16),
            pltpu.SemaphoreType.DMA((NX,)),
        ],
        compiler_params=pltpu.CompilerParams(vmem_limit_bytes=24 * 1024 * 1024),
        cost_estimate=pl.CostEstimate(flops=2 * 10**9, bytes_accessed=2**21, transcendentals=2**21),
        name="grads",
    )(live, work, qg, *kv, far, stats)


def finish_kernel(total_ref, arrived_ref, dk_ref, dv_ref):
    dk_ref[...] = (total_ref[0, 0] + arrived_ref[0].astype(jnp.float32)).astype(jnp.bfloat16)
    dv_ref[...] = (total_ref[0, 1] + arrived_ref[1].astype(jnp.float32)).astype(jnp.bfloat16)


def run_finish(total, arrived):
    return pl.pallas_call(
        finish_kernel,
        out_shape=[jax.ShapeDtypeStruct((HALF, HD), jnp.bfloat16)] * 2,
        in_specs=[VMEM] * 2,
        out_specs=[VMEM] * 2,
        compiler_params=pltpu.CompilerParams(vmem_limit_bytes=8 * 1024 * 1024),
        cost_estimate=pl.CostEstimate(flops=10**11, bytes_accessed=2**20, transcendentals=0),
        name="finish",
    )(total, arrived)


def sum_kernel(parts_ref, dq_ref):
    dq = parts_ref[0].astype(jnp.float32)
    for j in range(1, BLOCKS):
        dq = dq + parts_ref[j].astype(jnp.float32)
    dq_ref[...] = dq.astype(jnp.bfloat16)


def run_sum(parts):
    return pl.pallas_call(
        sum_kernel,
        out_shape=jax.ShapeDtypeStruct((HALF, HD), jnp.bfloat16),
        in_specs=[VMEM],
        out_specs=VMEM,
        compiler_params=pltpu.CompilerParams(vmem_limit_bytes=8 * 1024 * 1024),
        name="sum",
    )(parts)


def on_device(queries, keys, values, grad_out, key_tiles, work_lists):
    own_qg = jnp.stack([queries[0, 0], grad_out[0, 0]])
    mate_qg = flipped(own_qg, "p")
    own_kv = jnp.stack([keys[0, 0], values[0, 0]])
    across_kv = across(own_kv)
    spread = run_spread(own_qg, mate_qg)
    all_qg = lax.all_to_all(spread, "x", 0, 0)
    far, live = run_masks(key_tiles, spread)
    own_kv, _ = lax.optimization_barrier((own_kv, far))
    kv = (lax.all_gather(own_kv, "c"), lax.all_gather(across_kv, "c"))
    work = work_lists.reshape(16, 64)

    stats = run_stats(live, all_qg, kv, far)
    stats = lax.all_to_all(stats, ("x", "p"), 0, 0)
    keep, send, dq = run_grads(live, work, all_qg, kv, far, stats)

    total = keep + flipped(send, "c").astype(jnp.float32)
    dkv_out = total[1].astype(jnp.bfloat16)
    dkv_out, dq = lax.optimization_barrier((dkv_out, dq))
    from_across = across(dkv_out)
    dq = dq.reshape(BLOCKS, HALF, HD)
    dq_parts = lax.all_to_all(dq, ("x", "p"), 0, 0)
    grad_keys, grad_values = run_finish(total, from_across)
    outs = (run_sum(dq_parts), grad_keys, grad_values)
    return tuple(out[None, None] for out in outs)


def solution(mesh):
    devices = mesh.devices.reshape(4, 2, 2, 16, 2)
    fine = Mesh(devices, ("x", "zh", "c", "n", "p"))
    spec = P(("x", "zh", "c"), ("n", "p"), None, None)
    return jax.shard_map(
        on_device,
        mesh=fine,
        in_specs=(spec, spec, spec, spec, P(), P()),
        out_specs=(spec, spec, spec),
        check_vma=False,
    )
```

```python
import functools

import jax
import jax.numpy as jnp
from jax import lax
from jax.experimental import pallas as pl
from jax.experimental.pallas import tpu as pltpu
from jax.sharding import Mesh, PartitionSpec as P

TILE = 128
HD = 128
HALF = 256
NX = 4
NCHUNK = 4
BLOCKS = 2 * NX
ROWS = BLOCKS * HALF
SCALE = HD**-0.5
SCALE2 = SCALE * 1.4426950408889634
FAR = 1e30


def dot_t(a, b):
    return lax.dot_general(a, b, (((1,), (1,)), ((), ())), preferred_element_type=jnp.float32)


def dot_n(a, b):
    return jnp.dot(a, b, preferred_element_type=jnp.float32)


def spread_kernel(own_ref, mate_ref, out_ref):
    half = lax.axis_index("p")
    for j in range(NX):
        out_ref[j, half] = own_ref[...]
        out_ref[j, 1 - half] = mate_ref[...]


def mask_kernel(tiles_ref, after_ref, far_ref, live_ref, table_ref):
    x, zh, core, half = (lax.axis_index(name) for name in ("x", "zh", "c", "p"))
    tiles = tiles_ref[...]
    for k in range(2 * NCHUNK):
        chunk_zh = zh if k // 4 == 0 else 1 - zh
        chunk_half = half if k // 4 == 0 else 1 - half
        key_id = (4 * x + 2 * chunk_zh + k // 2 % 2) * 4 + 2 * chunk_half + k % 2
        hit = jnp.where(tiles == key_id, 0.0, FAR)
        table_ref[k] = jnp.broadcast_to(jnp.min(hit, axis=1, keepdims=True), (64, TILE))
    for n in range(NX):
        first = (4 * n + 2 * zh + core) * 4
        for side in range(2):
            nearest = jnp.full((4, TILE), FAR, jnp.float32)
            for k in range(NCHUNK * side, NCHUNK * (side + 1)):
                four = table_ref[k, pl.ds(first, 4), :]
                nearest = jnp.minimum(nearest, four)
                for h in range(2):
                    far_ref[n, h, k : k + 1, :TILE] = four[2 * h : 2 * h + 1]
                    far_ref[n, h, k : k + 1, TILE:] = four[2 * h + 1 : 2 * h + 2]
            live_ref[2 * n + side] = (jnp.min(nearest) < 1.0).astype(jnp.int32)


def by_sides(live_ref, n, work, nothing):
    here, there = live_ref[2 * n], live_ref[2 * n + 1]
    pl.when((here > 0) & (there > 0))(lambda: work((0, 1, 2, 3)))
    pl.when((here > 0) & (there == 0))(lambda: work((0, 1)))
    pl.when((here == 0) & (there > 0))(lambda: work((2, 3)))
    pl.when((here == 0) & (there == 0))(nothing)


def stats_kernel(live_ref, qg_ref, here_ref, there_ref, far_ref, out_ref):
    chunks = (here_ref.at[0], here_ref.at[1], there_ref.at[0], there_ref.at[1])

    def group(n, carry):
        def work(subset):
            for h in range(2):
                q = qg_ref[n, h, 0]
                g = qg_ref[n, h, 1]
                far = far_ref[n, h]
                scores = {}
                top = jnp.full((1, HALF), -FAR, jnp.float32)
                for i in subset:
                    s = dot_t(chunks[i][0], q)
                    for t in range(2):
                        k = 2 * i + t
                        scores[k] = s[t * TILE : (t + 1) * TILE]
                        near = jnp.max(scores[k], axis=0, keepdims=True) - far[k : k + 1]
                        top = jnp.maximum(top, near)
                top = top * SCALE2
                total = jnp.zeros((1, HALF), jnp.float32)
                weighted = jnp.zeros((1, HALF), jnp.float32)
                for i in subset:
                    gp = dot_t(chunks[i][1], g)
                    for t in range(2):
                        k = 2 * i + t
                        e = jnp.exp2(scores[k] * SCALE2 - (top + 4.0 * far[k : k + 1]))
                        total = total + jnp.sum(e, axis=0, keepdims=True)
                        weighted = weighted + jnp.sum(
                            e * gp[t * TILE : (t + 1) * TILE], axis=0, keepdims=True
                        )
                some = total > 0.0
                safe = jnp.where(some, total, 1.0)
                lse = jnp.where(some, top + jnp.log2(safe), -FAR)
                mean = jnp.where(some, weighted / safe, 0.0)
                for j in range(BLOCKS):
                    out_ref[j, n, h, :, :HALF] = lse
                    out_ref[j, n, h, :, HALF:] = mean

        def nothing():
            for j in range(BLOCKS):
                for h in range(2):
                    out_ref[j, n, h, :, :HALF] = jnp.full((1, HALF), -FAR, jnp.float32)
                    out_ref[j, n, h, :, HALF:] = jnp.zeros((1, HALF), jnp.float32)

        by_sides(live_ref, n, work, nothing)
        return carry

    lax.fori_loop(0, NX, group, 0)


def turn_kernel(here_ref, there_ref, after_ref, kt_ref):
    chunks = (here_ref.at[0], here_ref.at[1], there_ref.at[0], there_ref.at[1])
    for i, chunk in enumerate(chunks):
        kt_ref[:, i * HALF : (i + 1) * HALF] = chunk[0].T


def grads_kernel(
    live_ref,
    work_ref,
    qg_ref,
    here_ref,
    there_ref,
    far_ref,
    stats_ref,
    kt_ref,
    keep_ref,
    send_here_ref,
    send_there_ref,
    dq_ref,
    dk_acc,
    dv_acc,
    ds_ref,
    dq_buf,
    sems,
):
    zh, core, head = (lax.axis_index(name) for name in ("zh", "c", "n"))
    chunks = (here_ref.at[0], here_ref.at[1], there_ref.at[0], there_ref.at[1])
    dk_acc[...] = jnp.zeros_like(dk_acc)
    dv_acc[...] = jnp.zeros_like(dv_acc)

    def group(n, carry):
        def work(subset):
            q_all = qg_ref[n, :, 0].reshape(2 * HALF, HD)
            g_all = qg_ref[n, :, 1].reshape(2 * HALF, HD)
            rows_stats = []
            for h in range(2):
                lse_parts = [stats_ref[j, n, h, :, :HALF] for j in range(BLOCKS)]
                top = functools.reduce(jnp.maximum, lse_parts)
                total = jnp.zeros((1, HALF), jnp.float32)
                weighted = jnp.zeros((1, HALF), jnp.float32)
                for j in range(BLOCKS):
                    w = jnp.exp2(lse_parts[j] - top)
                    total = total + w
                    weighted = weighted + w * stats_ref[j, n, h, :, HALF:]
                rows_stats.append((top + jnp.log2(total), weighted / total))
            for i in subset:
                rows = slice(i * HALF, (i + 1) * HALF)
                ps, ds = [], []
                for h in range(2):
                    lse, delta = rows_stats[h]
                    s = dot_t(chunks[i][0], qg_ref[n, h, 0])
                    gp = dot_t(chunks[i][1], qg_ref[n, h, 1])
                    p_parts, d_parts = [], []
                    for t in range(2):
                        k = 2 * i + t
                        part = slice(t * TILE, (t + 1) * TILE)
                        shift = lse + 4.0 * far_ref[n, h, k : k + 1, :]
                        p = jnp.exp2(s[part] * SCALE2 - shift)
                        p_parts.append(p.astype(jnp.bfloat16))
                        d_parts.append((p * (gp[part] - delta)).astype(jnp.bfloat16))
                    ps.append(jnp.concatenate(p_parts, axis=0))
                    d = jnp.concatenate(d_parts, axis=0)
                    ds.append(d)
                    ds_ref[h, rows] = d
                dv_acc[rows] += dot_n(jnp.concatenate(ps, axis=1), g_all)
                dk_acc[rows] += dot_n(jnp.concatenate(ds, axis=1), q_all)
            used = slice(subset[0] * HALF, (subset[-1] + 1) * HALF)
            for h in range(2):
                dq = (dot_n(kt_ref[:, used], ds_ref[h, used]) * SCALE).T.astype(jnp.bfloat16)
                for t in range(2):
                    slot = jnp.int32(3)
                    for w in range(3):
                        listed = work_ref[4 * n + 2 * zh + core, 4 * head + w]
                        slot = jnp.where(listed == 2 * h + t, w, slot)
                    dq_buf[n, slot] = dq[t * TILE : (t + 1) * TILE]

        def nothing():
            dq_buf[n] = jnp.zeros((4, TILE, HD), jnp.bfloat16)

        by_sides(live_ref, n, work, nothing)
        pltpu.make_async_copy(dq_buf.at[n], dq_ref.at[n], sems.at[n]).start()
        return carry

    lax.fori_loop(0, NX, group, 0)
    for i, send_ref in enumerate((send_here_ref, send_there_ref)):
        rows = pl.ds((2 * i + core) * HALF, HALF)
        keep_ref[i, 0] = dk_acc[rows] * SCALE
        keep_ref[i, 1] = dv_acc[rows]
        rows = pl.ds((2 * i + 1 - core) * HALF, HALF)
        send_ref[0] = (dk_acc[rows] * SCALE).astype(jnp.bfloat16)
        send_ref[1] = dv_acc[rows].astype(jnp.bfloat16)
    for n in range(NX):
        pltpu.make_async_copy(dq_buf.at[n], dq_ref.at[n], sems.at[n]).wait()


VMEM = pl.BlockSpec(memory_space=pltpu.VMEM)
SMEM = pl.BlockSpec(memory_space=pltpu.SMEM)


def flipped(value, axis):
    return lax.ppermute(value, axis, [(0, 1), (1, 0)])


def across(value):
    return lax.ppermute(value, ("zh", "p"), [(0, 3), (1, 2), (2, 1), (3, 0)])


def run_spread(own, mate):
    return pl.pallas_call(
        spread_kernel,
        out_shape=jax.ShapeDtypeStruct((NX, 2) + own.shape, own.dtype),
        in_specs=[VMEM] * 2,
        out_specs=VMEM,
        compiler_params=pltpu.CompilerParams(vmem_limit_bytes=8 * 1024 * 1024),
        name="spread",
    )(own, mate)


def run_masks(tiles, after):
    return pl.pallas_call(
        mask_kernel,
        out_shape=[
            jax.ShapeDtypeStruct((NX, 2, 2 * NCHUNK, HALF), jnp.float32),
            jax.ShapeDtypeStruct((2 * NX,), jnp.int32),
        ],
        in_specs=[VMEM, pl.BlockSpec(memory_space=pl.ANY)],
        out_specs=[VMEM, SMEM],
        scratch_shapes=[pltpu.VMEM((2 * NCHUNK, 64, TILE), jnp.float32)],
        compiler_params=pltpu.CompilerParams(vmem_limit_bytes=8 * 1024 * 1024),
        cost_estimate=pl.CostEstimate(flops=10**10, bytes_accessed=2**20, transcendentals=0),
        name="masks",
    )(tiles, after)


def run_stats(live, qg, kv, far):
    return pl.pallas_call(
        stats_kernel,
        out_shape=jax.ShapeDtypeStruct((BLOCKS, NX, 2, 1, 2 * HALF), jnp.float32),
        in_specs=[SMEM] + [VMEM] * 4,
        out_specs=VMEM,
        compiler_params=pltpu.CompilerParams(vmem_limit_bytes=32 * 1024 * 1024),
        cost_estimate=pl.CostEstimate(flops=10**9, bytes_accessed=2**21, transcendentals=2**21),
        name="stats",
    )(live, qg, *kv, far)


def run_turn(kv, after):
    return pl.pallas_call(
        turn_kernel,
        out_shape=jax.ShapeDtypeStruct((HD, NCHUNK * HALF), jnp.bfloat16),
        in_specs=[VMEM, VMEM, pl.BlockSpec(memory_space=pl.ANY)],
        out_specs=VMEM,
        compiler_params=pltpu.CompilerParams(vmem_limit_bytes=8 * 1024 * 1024),
        cost_estimate=pl.CostEstimate(flops=10**9, bytes_accessed=2**20, transcendentals=0),
        name="turn",
    )(*kv, after)


def run_grads(live, work, qg, kv, far, stats, kt):
    return pl.pallas_call(
        grads_kernel,
        out_shape=[
            jax.ShapeDtypeStruct((2, 2, HALF, HD), jnp.float32),
            jax.ShapeDtypeStruct((2, HALF, HD), jnp.bfloat16),
            jax.ShapeDtypeStruct((2, HALF, HD), jnp.bfloat16),
            jax.ShapeDtypeStruct((NX, 4, TILE, HD), jnp.bfloat16),
        ],
        in_specs=[SMEM, SMEM] + [VMEM] * 6,
        out_specs=[VMEM, VMEM, VMEM, pl.BlockSpec(memory_space=pl.ANY)],
        scratch_shapes=[
            pltpu.VMEM((NCHUNK * HALF, HD), jnp.float32),
            pltpu.VMEM((NCHUNK * HALF, HD), jnp.float32),
            pltpu.VMEM((2, NCHUNK * HALF, HALF), jnp.bfloat16),
            pltpu.VMEM((NX, 4, TILE, HD), jnp.bfloat16),
            pltpu.SemaphoreType.DMA((NX,)),
        ],
        compiler_params=pltpu.CompilerParams(vmem_limit_bytes=24 * 1024 * 1024),
        cost_estimate=pl.CostEstimate(flops=2 * 10**9, bytes_accessed=2**21, transcendentals=2**21),
        name="grads",
    )(live, work, qg, *kv, far, stats, kt)


def finish_kernel(keep_ref, sibling_ref, arrived_ref, dk_ref, dv_ref):
    for i, out_ref in enumerate((dk_ref, dv_ref)):
        total = keep_ref[0, i] + sibling_ref[i].astype(jnp.float32)
        out_ref[...] = (total + arrived_ref[i].astype(jnp.float32)).astype(jnp.bfloat16)


def run_finish(keep, sibling, arrived):
    return pl.pallas_call(
        finish_kernel,
        out_shape=[jax.ShapeDtypeStruct((HALF, HD), jnp.bfloat16)] * 2,
        in_specs=[VMEM] * 3,
        out_specs=[VMEM] * 2,
        compiler_params=pltpu.CompilerParams(vmem_limit_bytes=8 * 1024 * 1024),
        cost_estimate=pl.CostEstimate(flops=10**11, bytes_accessed=2**20, transcendentals=0),
        name="finish",
    )(keep, sibling, arrived)


def sum_kernel(parts_ref, dq_ref):
    dq = parts_ref[0].astype(jnp.float32)
    for j in range(1, BLOCKS):
        dq = dq + parts_ref[j].astype(jnp.float32)
    dq_ref[...] = dq.astype(jnp.bfloat16)


def run_sum(parts):
    return pl.pallas_call(
        sum_kernel,
        out_shape=jax.ShapeDtypeStruct((HALF, HD), jnp.bfloat16),
        in_specs=[VMEM],
        out_specs=VMEM,
        compiler_params=pltpu.CompilerParams(vmem_limit_bytes=8 * 1024 * 1024),
        name="sum",
    )(parts)


def on_device(queries, keys, values, grad_out, key_tiles, work_lists):
    own_qg = jnp.stack([queries[0, 0], grad_out[0, 0]])
    mate_qg = flipped(own_qg, "p")
    own_kv = jnp.stack([keys[0, 0], values[0, 0]])
    across_kv = across(own_kv)
    spread = run_spread(own_qg, mate_qg)
    all_qg = lax.all_to_all(spread, "x", 0, 0)
    far, live = run_masks(key_tiles, spread)
    own_kv, _ = lax.optimization_barrier((own_kv, far))
    kv = (lax.all_gather(own_kv, "c"), lax.all_gather(across_kv, "c"))
    work = work_lists.reshape(16, 64)

    own_stats = run_stats(live, all_qg, kv, far)
    kt = run_turn(kv, own_stats)
    stats = lax.all_to_all(own_stats, ("x", "p"), 0, 0)
    keep, send_here, send_there, dq = run_grads(live, work, all_qg, kv, far, stats, kt)

    sibling = 1 - lax.axis_index("c")
    there = lax.dynamic_index_in_dim(lax.all_gather(send_there, "c"), sibling, 0, False)
    dkv_out = (keep[1] + there.astype(jnp.float32)).astype(jnp.bfloat16)
    dkv_out, dq, send_here = lax.optimization_barrier((dkv_out, dq, send_here))
    from_across = across(dkv_out)
    dq_parts = lax.all_to_all(dq.reshape(BLOCKS, HALF, HD), ("x", "p"), 0, 0)
    here = lax.dynamic_index_in_dim(lax.all_gather(send_here, "c"), sibling, 0, False)
    grad_keys, grad_values = run_finish(keep, here, from_across)
    outs = (run_sum(dq_parts), grad_keys, grad_values)
    return tuple(out[None, None] for out in outs)


def solution(mesh):
    devices = mesh.devices.reshape(4, 2, 2, 16, 2)
    fine = Mesh(devices, ("x", "zh", "c", "n", "p"))
    spec = P(("x", "zh", "c"), ("n", "p"), None, None)
    return jax.shard_map(
        on_device,
        mesh=fine,
        in_specs=(spec, spec, spec, spec, P(), P()),
        out_specs=(spec, spec, spec),
        check_vma=False,
    )
```

```python
import functools

import jax
import jax.numpy as jnp
from jax import lax
from jax.experimental import pallas as pl
from jax.experimental.pallas import tpu as pltpu
from jax.sharding import Mesh, PartitionSpec as P

TILE = 128
HD = 128
HALF = 256
NX = 4
NCHUNK = 4
BLOCKS = 2 * NX
ROWS = BLOCKS * HALF
SCALE = HD**-0.5
SCALE2 = SCALE * 1.4426950408889634
FAR = 1e30


def dot_t(a, b):
    return lax.dot_general(a, b, (((1,), (1,)), ((), ())), preferred_element_type=jnp.float32)


def dot_n(a, b):
    return jnp.dot(a, b, preferred_element_type=jnp.float32)


def spread_kernel(own_ref, mate_ref, out_ref):
    half = lax.axis_index("p")
    for j in range(NX):
        out_ref[j, half] = own_ref[...]
        out_ref[j, 1 - half] = mate_ref[...]


def mask_kernel(tiles_ref, after_ref, far_ref, live_ref, table_ref):
    x, zh, core, half = (lax.axis_index(name) for name in ("x", "zh", "c", "p"))
    tiles = tiles_ref[...]
    for k in range(2 * NCHUNK):
        chunk_zh = zh if k // 4 == 0 else 1 - zh
        chunk_half = half if k // 4 == 0 else 1 - half
        key_id = (4 * x + 2 * chunk_zh + k // 2 % 2) * 4 + 2 * chunk_half + k % 2
        hit = jnp.where(tiles == key_id, 0.0, FAR)
        table_ref[k] = jnp.broadcast_to(jnp.min(hit, axis=1, keepdims=True), (64, TILE))
    for n in range(NX):
        first = (4 * n + 2 * zh + core) * 4
        for side in range(2):
            nearest = jnp.full((4, TILE), FAR, jnp.float32)
            for k in range(NCHUNK * side, NCHUNK * (side + 1)):
                four = table_ref[k, pl.ds(first, 4), :]
                nearest = jnp.minimum(nearest, four)
                for h in range(2):
                    far_ref[n, h, k : k + 1, :TILE] = four[2 * h : 2 * h + 1]
                    far_ref[n, h, k : k + 1, TILE:] = four[2 * h + 1 : 2 * h + 2]
            live_ref[2 * n + side] = (jnp.min(nearest) < 1.0).astype(jnp.int32)


def by_sides(live_ref, n, work, nothing):
    here, there = live_ref[2 * n], live_ref[2 * n + 1]
    pl.when((here > 0) & (there > 0))(lambda: work((0, 1, 2, 3)))
    pl.when((here > 0) & (there == 0))(lambda: work((0, 1)))
    pl.when((here == 0) & (there > 0))(lambda: work((2, 3)))
    pl.when((here == 0) & (there == 0))(nothing)


def stats_kernel(live_ref, qg_ref, here_ref, there_ref, far_ref, out_ref):
    chunks = (here_ref.at[0], here_ref.at[1], there_ref.at[0], there_ref.at[1])

    def group(n, carry):
        def work(subset):
            for h in range(2):
                q = qg_ref[n, h, 0]
                g = qg_ref[n, h, 1]
                far = far_ref[n, h]
                scores = {}
                top = jnp.full((1, HALF), -FAR, jnp.float32)
                for i in subset:
                    s = dot_t(chunks[i][0], q)
                    for t in range(2):
                        k = 2 * i + t
                        scores[k] = s[t * TILE : (t + 1) * TILE]
                        near = jnp.max(scores[k], axis=0, keepdims=True) - far[k : k + 1]
                        top = jnp.maximum(top, near)
                top = top * SCALE2
                total = jnp.zeros((1, HALF), jnp.float32)
                weighted = jnp.zeros((1, HALF), jnp.float32)
                for i in subset:
                    gp = dot_t(chunks[i][1], g)
                    for t in range(2):
                        k = 2 * i + t
                        e = jnp.exp2(scores[k] * SCALE2 - (top + 4.0 * far[k : k + 1]))
                        total = total + jnp.sum(e, axis=0, keepdims=True)
                        weighted = weighted + jnp.sum(
                            e * gp[t * TILE : (t + 1) * TILE], axis=0, keepdims=True
                        )
                some = total > 0.0
                safe = jnp.where(some, total, 1.0)
                lse = jnp.where(some, top + jnp.log2(safe), -FAR)
                mean = jnp.where(some, weighted / safe, 0.0)
                for j in range(BLOCKS):
                    out_ref[j, n, h, :, :HALF] = lse
                    out_ref[j, n, h, :, HALF:] = mean

        def nothing():
            for j in range(BLOCKS):
                for h in range(2):
                    out_ref[j, n, h, :, :HALF] = jnp.full((1, HALF), -FAR, jnp.float32)
                    out_ref[j, n, h, :, HALF:] = jnp.zeros((1, HALF), jnp.float32)

        by_sides(live_ref, n, work, nothing)
        return carry

    lax.fori_loop(0, NX, group, 0)


def turn_kernel(here_ref, there_ref, after_ref, kt_ref):
    chunks = (here_ref.at[0], here_ref.at[1], there_ref.at[0], there_ref.at[1])
    for i, chunk in enumerate(chunks):
        kt_ref[:, i * HALF : (i + 1) * HALF] = chunk[0].T


def side_grads(side, n, qg_ref, keys_ref, far_ref, stats_ref, kt_ref, dk_acc, dv_acc, ds_ref):
    q_all = qg_ref[n, :, 0].reshape(2 * HALF, HD)
    g_all = qg_ref[n, :, 1].reshape(2 * HALF, HD)
    rows_stats = []
    for h in range(2):
        lse_parts = [stats_ref[j, n, h, :, :HALF] for j in range(BLOCKS)]
        top = functools.reduce(jnp.maximum, lse_parts)
        total = jnp.zeros((1, HALF), jnp.float32)
        weighted = jnp.zeros((1, HALF), jnp.float32)
        for j in range(BLOCKS):
            w = jnp.exp2(lse_parts[j] - top)
            total = total + w
            weighted = weighted + w * stats_ref[j, n, h, :, HALF:]
        rows_stats.append((top + jnp.log2(total), weighted / total))
    for i in range(2):
        rows = slice(i * HALF, (i + 1) * HALF)
        ps, ds = [], []
        for h in range(2):
            lse, delta = rows_stats[h]
            s = dot_t(keys_ref[i, 0], qg_ref[n, h, 0])
            gp = dot_t(keys_ref[i, 1], qg_ref[n, h, 1])
            p_parts, d_parts = [], []
            for t in range(2):
                k = NCHUNK * side + 2 * i + t
                part = slice(t * TILE, (t + 1) * TILE)
                shift = lse + 4.0 * far_ref[n, h, k : k + 1, :]
                p = jnp.exp2(s[part] * SCALE2 - shift)
                p_parts.append(p.astype(jnp.bfloat16))
                d_parts.append((p * (gp[part] - delta)).astype(jnp.bfloat16))
            ps.append(jnp.concatenate(p_parts, axis=0))
            d = jnp.concatenate(d_parts, axis=0)
            ds.append(d)
            ds_ref[h, rows] = d
        dv_acc[rows] += dot_n(jnp.concatenate(ps, axis=1), g_all)
        dk_acc[rows] += dot_n(jnp.concatenate(ds, axis=1), q_all)
    used = slice(2 * side * HALF, 2 * (side + 1) * HALF)
    return [dot_n(kt_ref[:, used], ds_ref[h]) for h in range(2)]


def split_keys(core, dk_acc, dv_acc, keep_ref, send_ref):
    rows = pl.ds(core * HALF, HALF)
    keep_ref[0] = dk_acc[rows] * SCALE
    keep_ref[1] = dv_acc[rows]
    rows = pl.ds((1 - core) * HALF, HALF)
    send_ref[0] = (dk_acc[rows] * SCALE).astype(jnp.bfloat16)
    send_ref[1] = dv_acc[rows].astype(jnp.bfloat16)


def there_kernel(
    live_ref,
    qg_ref,
    there_ref,
    far_ref,
    stats_ref,
    kt_ref,
    keep_ref,
    send_ref,
    dqt_ref,
    dk_acc,
    dv_acc,
    ds_ref,
):
    dk_acc[...] = jnp.zeros_like(dk_acc)
    dv_acc[...] = jnp.zeros_like(dv_acc)

    def group(n, carry):
        @pl.when(live_ref[2 * n + 1] > 0)
        def _():
            parts = side_grads(
                1, n, qg_ref, there_ref, far_ref, stats_ref, kt_ref, dk_acc, dv_acc, ds_ref
            )
            for h in range(2):
                dqt_ref[n, h] = parts[h]

        @pl.when(live_ref[2 * n + 1] == 0)
        def _():
            dqt_ref[n] = jnp.zeros((2, HD, HALF), jnp.float32)

        return carry

    lax.fori_loop(0, NX, group, 0)
    split_keys(lax.axis_index("c"), dk_acc, dv_acc, keep_ref, send_ref)


def here_kernel(
    live_ref,
    work_ref,
    qg_ref,
    here_ref,
    far_ref,
    stats_ref,
    kt_ref,
    dqt_ref,
    after_ref,
    keep_ref,
    send_ref,
    dq_ref,
    dk_acc,
    dv_acc,
    ds_ref,
    dq_buf,
    sems,
):
    zh, core, head = (lax.axis_index(name) for name in ("zh", "c", "n"))
    dk_acc[...] = jnp.zeros_like(dk_acc)
    dv_acc[...] = jnp.zeros_like(dv_acc)

    def group(n, carry):
        def deliver(parts):
            for h in range(2):
                dq = (parts[h] * SCALE).T.astype(jnp.bfloat16)
                for t in range(2):
                    slot = jnp.int32(3)
                    for w in range(3):
                        listed = work_ref[4 * n + 2 * zh + core, 4 * head + w]
                        slot = jnp.where(listed == 2 * h + t, w, slot)
                    dq_buf[n, slot] = dq[t * TILE : (t + 1) * TILE]

        @pl.when(live_ref[2 * n] > 0)
        def _():
            parts = side_grads(
                0, n, qg_ref, here_ref, far_ref, stats_ref, kt_ref, dk_acc, dv_acc, ds_ref
            )
            deliver([parts[h] + dqt_ref[n, h] for h in range(2)])

        @pl.when(live_ref[2 * n] == 0)
        def _():
            deliver([dqt_ref[n, h] for h in range(2)])

        pltpu.make_async_copy(dq_buf.at[n], dq_ref.at[n], sems.at[n]).start()
        return carry

    lax.fori_loop(0, NX, group, 0)
    split_keys(core, dk_acc, dv_acc, keep_ref, send_ref)
    for n in range(NX):
        pltpu.make_async_copy(dq_buf.at[n], dq_ref.at[n], sems.at[n]).wait()


VMEM = pl.BlockSpec(memory_space=pltpu.VMEM)
SMEM = pl.BlockSpec(memory_space=pltpu.SMEM)


def flipped(value, axis):
    return lax.ppermute(value, axis, [(0, 1), (1, 0)])


def across(value):
    return lax.ppermute(value, ("zh", "p"), [(0, 3), (1, 2), (2, 1), (3, 0)])


def run_spread(own, mate):
    return pl.pallas_call(
        spread_kernel,
        out_shape=jax.ShapeDtypeStruct((NX, 2) + own.shape, own.dtype),
        in_specs=[VMEM] * 2,
        out_specs=VMEM,
        compiler_params=pltpu.CompilerParams(vmem_limit_bytes=8 * 1024 * 1024),
        name="spread",
    )(own, mate)


def run_masks(tiles, after):
    return pl.pallas_call(
        mask_kernel,
        out_shape=[
            jax.ShapeDtypeStruct((NX, 2, 2 * NCHUNK, HALF), jnp.float32),
            jax.ShapeDtypeStruct((2 * NX,), jnp.int32),
        ],
        in_specs=[VMEM, pl.BlockSpec(memory_space=pl.ANY)],
        out_specs=[VMEM, SMEM],
        scratch_shapes=[pltpu.VMEM((2 * NCHUNK, 64, TILE), jnp.float32)],
        compiler_params=pltpu.CompilerParams(vmem_limit_bytes=8 * 1024 * 1024),
        cost_estimate=pl.CostEstimate(flops=10**10, bytes_accessed=2**20, transcendentals=0),
        name="masks",
    )(tiles, after)


def run_stats(live, qg, kv, far):
    return pl.pallas_call(
        stats_kernel,
        out_shape=jax.ShapeDtypeStruct((BLOCKS, NX, 2, 1, 2 * HALF), jnp.float32),
        in_specs=[SMEM] + [VMEM] * 4,
        out_specs=VMEM,
        compiler_params=pltpu.CompilerParams(vmem_limit_bytes=32 * 1024 * 1024),
        cost_estimate=pl.CostEstimate(flops=10**9, bytes_accessed=2**21, transcendentals=2**21),
        name="stats",
    )(live, qg, *kv, far)


def run_turn(kv, after):
    return pl.pallas_call(
        turn_kernel,
        out_shape=jax.ShapeDtypeStruct((HD, NCHUNK * HALF), jnp.bfloat16),
        in_specs=[VMEM, VMEM, pl.BlockSpec(memory_space=pl.ANY)],
        out_specs=VMEM,
        compiler_params=pltpu.CompilerParams(vmem_limit_bytes=8 * 1024 * 1024),
        cost_estimate=pl.CostEstimate(flops=10**9, bytes_accessed=2**20, transcendentals=0),
        name="turn",
    )(*kv, after)


ACCUMULATORS = [
    pltpu.VMEM((2 * HALF, HD), jnp.float32),
    pltpu.VMEM((2 * HALF, HD), jnp.float32),
    pltpu.VMEM((2, 2 * HALF, HALF), jnp.bfloat16),
]


def run_there(live, qg, there, far, stats, kt):
    return pl.pallas_call(
        there_kernel,
        out_shape=[
            jax.ShapeDtypeStruct((2, HALF, HD), jnp.float32),
            jax.ShapeDtypeStruct((2, HALF, HD), jnp.bfloat16),
            jax.ShapeDtypeStruct((NX, 2, HD, HALF), jnp.float32),
        ],
        in_specs=[SMEM] + [VMEM] * 5,
        out_specs=[VMEM] * 3,
        scratch_shapes=ACCUMULATORS,
        compiler_params=pltpu.CompilerParams(vmem_limit_bytes=24 * 1024 * 1024),
        cost_estimate=pl.CostEstimate(flops=10**9, bytes_accessed=2**21, transcendentals=2**20),
        name="there",
    )(live, qg, there, far, stats, kt)


def run_here(live, work, qg, here, far, stats, kt, dqt, after):
    anywhere = pl.BlockSpec(memory_space=pl.ANY)
    return pl.pallas_call(
        here_kernel,
        out_shape=[
            jax.ShapeDtypeStruct((2, HALF, HD), jnp.float32),
            jax.ShapeDtypeStruct((2, HALF, HD), jnp.bfloat16),
            jax.ShapeDtypeStruct((NX, 4, TILE, HD), jnp.bfloat16),
        ],
        in_specs=[SMEM, SMEM] + [VMEM] * 6 + [anywhere],
        out_specs=[VMEM, VMEM, anywhere],
        scratch_shapes=ACCUMULATORS
        + [pltpu.VMEM((NX, 4, TILE, HD), jnp.bfloat16), pltpu.SemaphoreType.DMA((NX,))],
        compiler_params=pltpu.CompilerParams(vmem_limit_bytes=24 * 1024 * 1024),
        cost_estimate=pl.CostEstimate(flops=10**11, bytes_accessed=2**21, transcendentals=2**20),
        name="here",
    )(live, work, qg, here, far, stats, kt, dqt, after)


def finish_kernel(keep_ref, sibling_ref, arrived_ref, dk_ref, dv_ref):
    for i, out_ref in enumerate((dk_ref, dv_ref)):
        total = keep_ref[i] + sibling_ref[i].astype(jnp.float32)
        out_ref[...] = (total + arrived_ref[i].astype(jnp.float32)).astype(jnp.bfloat16)


def run_finish(keep, sibling, arrived):
    return pl.pallas_call(
        finish_kernel,
        out_shape=[jax.ShapeDtypeStruct((HALF, HD), jnp.bfloat16)] * 2,
        in_specs=[VMEM] * 3,
        out_specs=[VMEM] * 2,
        compiler_params=pltpu.CompilerParams(vmem_limit_bytes=8 * 1024 * 1024),
        cost_estimate=pl.CostEstimate(flops=10**11, bytes_accessed=2**20, transcendentals=0),
        name="finish",
    )(keep, sibling, arrived)


def sum_kernel(parts_ref, dq_ref):
    dq = parts_ref[0].astype(jnp.float32)
    for j in range(1, BLOCKS):
        dq = dq + parts_ref[j].astype(jnp.float32)
    dq_ref[...] = dq.astype(jnp.bfloat16)


def run_sum(parts):
    return pl.pallas_call(
        sum_kernel,
        out_shape=jax.ShapeDtypeStruct((HALF, HD), jnp.bfloat16),
        in_specs=[VMEM],
        out_specs=VMEM,
        compiler_params=pltpu.CompilerParams(vmem_limit_bytes=8 * 1024 * 1024),
        name="sum",
    )(parts)


def on_device(queries, keys, values, grad_out, key_tiles, work_lists):
    own_qg = jnp.stack([queries[0, 0], grad_out[0, 0]])
    mate_qg = flipped(own_qg, "p")
    own_kv = jnp.stack([keys[0, 0], values[0, 0]])
    across_kv = across(own_kv)
    spread = run_spread(own_qg, mate_qg)
    all_qg = lax.all_to_all(spread, "x", 0, 0)
    far, live = run_masks(key_tiles, spread)
    own_kv, _ = lax.optimization_barrier((own_kv, far))
    kv = (lax.all_gather(own_kv, "c"), lax.all_gather(across_kv, "c"))
    work = work_lists.reshape(16, 64)

    own_stats = run_stats(live, all_qg, kv, far)
    kt = run_turn(kv, own_stats)
    stats = lax.all_to_all(own_stats, ("x", "p"), 0, 0)
    sibling = 1 - lax.axis_index("c")
    keep_there, send_there, dqt = run_there(live, all_qg, kv[1], far, stats, kt)
    there = lax.dynamic_index_in_dim(lax.all_gather(send_there, "c"), sibling, 0, False)
    dkv_out = (keep_there + there.astype(jnp.float32)).astype(jnp.bfloat16)
    from_across = across(dkv_out)
    keep, send, dq = run_here(live, work, all_qg, kv[0], far, stats, kt, dqt, dkv_out)
    dq_parts = lax.all_to_all(dq.reshape(BLOCKS, HALF, HD), ("x", "p"), 0, 0)
    here = lax.dynamic_index_in_dim(lax.all_gather(send, "c"), sibling, 0, False)
    grad_keys, grad_values = run_finish(keep, here, from_across)
    outs = (run_sum(dq_parts), grad_keys, grad_values)
    return tuple(out[None, None] for out in outs)


def solution(mesh):
    devices = mesh.devices.reshape(4, 2, 2, 16, 2)
    fine = Mesh(devices, ("x", "zh", "c", "n", "p"))
    spec = P(("x", "zh", "c"), ("n", "p"), None, None)
    return jax.shard_map(
        on_device,
        mesh=fine,
        in_specs=(spec, spec, spec, spec, P(), P()),
        out_specs=(spec, spec, spec),
        check_vma=False,
    )
```

```python
import functools

import jax
import jax.numpy as jnp
from jax import lax
from jax.experimental import pallas as pl
from jax.experimental.pallas import tpu as pltpu
from jax.sharding import Mesh, PartitionSpec as P

TILE = 128
HD = 128
HALF = 256
NX = 4
NCHUNK = 4
BLOCKS = 2 * NX
ROWS = BLOCKS * HALF
SCALE = HD**-0.5
SCALE2 = SCALE * 1.4426950408889634
FAR = 1e30


def dot_t(a, b):
    return lax.dot_general(a, b, (((1,), (1,)), ((), ())), preferred_element_type=jnp.float32)


def dot_n(a, b):
    return jnp.dot(a, b, preferred_element_type=jnp.float32)


def spread_kernel(own_ref, mate_ref, out_ref, sems):
    half = lax.axis_index("p")
    copies = []
    for j in range(NX):
        for i, (source, index) in enumerate(((own_ref, half), (mate_ref, 1 - half))):
            target = out_ref.at[j, index]
            copies.append(pltpu.make_async_copy(source, target, sems.at[2 * j + i]))
    for copy in copies:
        copy.start()
    for copy in copies:
        copy.wait()


def mask_kernel(tiles_ref, after_ref, far_ref, live_ref, table_ref):
    x, zh, core, half = (lax.axis_index(name) for name in ("x", "zh", "c", "p"))
    tiles = tiles_ref[...]
    for k in range(2 * NCHUNK):
        chunk_zh = zh if k // 4 == 0 else 1 - zh
        chunk_half = half if k // 4 == 0 else 1 - half
        key_id = (4 * x + 2 * chunk_zh + k // 2 % 2) * 4 + 2 * chunk_half + k % 2
        hit = jnp.where(tiles == key_id, 0.0, FAR)
        table_ref[k] = jnp.broadcast_to(jnp.min(hit, axis=1, keepdims=True), (64, TILE))
    for n in range(NX):
        first = (4 * n + 2 * zh + core) * 4
        for side in range(2):
            nearest = jnp.full((4, TILE), FAR, jnp.float32)
            for k in range(NCHUNK * side, NCHUNK * (side + 1)):
                four = table_ref[k, pl.ds(first, 4), :]
                nearest = jnp.minimum(nearest, four)
                for h in range(2):
                    far_ref[n, h, k : k + 1, :TILE] = four[2 * h : 2 * h + 1]
                    far_ref[n, h, k : k + 1, TILE:] = four[2 * h + 1 : 2 * h + 2]
            live_ref[2 * n + side] = (jnp.min(nearest) < 1.0).astype(jnp.int32)


def by_sides(live_ref, n, work, nothing):
    here, there = live_ref[2 * n], live_ref[2 * n + 1]
    pl.when((here > 0) & (there > 0))(lambda: work((0, 1, 2, 3)))
    pl.when((here > 0) & (there == 0))(lambda: work((0, 1)))
    pl.when((here == 0) & (there > 0))(lambda: work((2, 3)))
    pl.when((here == 0) & (there == 0))(nothing)


def stats_kernel(live_ref, qg_ref, here_ref, there_ref, far_ref, out_ref):
    chunks = (here_ref.at[0], here_ref.at[1], there_ref.at[0], there_ref.at[1])

    def group(n, carry):
        def work(subset):
            for h in range(2):
                q = qg_ref[n, h, 0]
                g = qg_ref[n, h, 1]
                far = far_ref[n, h]
                scores = {}
                top = jnp.full((1, HALF), -FAR, jnp.float32)
                for i in subset:
                    s = dot_t(chunks[i][0], q)
                    for t in range(2):
                        k = 2 * i + t
                        scores[k] = s[t * TILE : (t + 1) * TILE]
                        near = jnp.max(scores[k], axis=0, keepdims=True) - far[k : k + 1]
                        top = jnp.maximum(top, near)
                top = top * SCALE2
                total = jnp.zeros((1, HALF), jnp.float32)
                weighted = jnp.zeros((1, HALF), jnp.float32)
                for i in subset:
                    gp = dot_t(chunks[i][1], g)
                    for t in range(2):
                        k = 2 * i + t
                        e = jnp.exp2(scores[k] * SCALE2 - (top + 4.0 * far[k : k + 1]))
                        total = total + jnp.sum(e, axis=0, keepdims=True)
                        weighted = weighted + jnp.sum(
                            e * gp[t * TILE : (t + 1) * TILE], axis=0, keepdims=True
                        )
                some = total > 0.0
                safe = jnp.where(some, total, 1.0)
                lse = jnp.where(some, top + jnp.log2(safe), -FAR)
                mean = jnp.where(some, weighted / safe, 0.0)
                for j in range(BLOCKS):
                    out_ref[j, n, h, :, :HALF] = lse
                    out_ref[j, n, h, :, HALF:] = mean

        def nothing():
            for j in range(BLOCKS):
                for h in range(2):
                    out_ref[j, n, h, :, :HALF] = jnp.full((1, HALF), -FAR, jnp.float32)
                    out_ref[j, n, h, :, HALF:] = jnp.zeros((1, HALF), jnp.float32)

        by_sides(live_ref, n, work, nothing)
        return carry

    lax.fori_loop(0, NX, group, 0)


def turn_kernel(here_ref, there_ref, after_ref, kt_ref):
    chunks = (here_ref.at[0], here_ref.at[1], there_ref.at[0], there_ref.at[1])
    for i, chunk in enumerate(chunks):
        kt_ref[:, i * HALF : (i + 1) * HALF] = chunk[0].T


def side_grads(side, n, qg_ref, keys_ref, far_ref, stats_ref, kt_ref, dk_acc, dv_acc, ds_ref):
    q_all = qg_ref[n, :, 0].reshape(2 * HALF, HD)
    g_all = qg_ref[n, :, 1].reshape(2 * HALF, HD)
    rows_stats = []
    for h in range(2):
        lse_parts = [stats_ref[j, n, h, :, :HALF] for j in range(BLOCKS)]
        top = functools.reduce(jnp.maximum, lse_parts)
        total = jnp.zeros((1, HALF), jnp.float32)
        weighted = jnp.zeros((1, HALF), jnp.float32)
        for j in range(BLOCKS):
            w = jnp.exp2(lse_parts[j] - top)
            total = total + w
            weighted = weighted + w * stats_ref[j, n, h, :, HALF:]
        rows_stats.append((top + jnp.log2(total), weighted / total))
    for i in range(2):
        rows = slice(i * HALF, (i + 1) * HALF)
        ps, ds = [], []
        for h in range(2):
            lse, delta = rows_stats[h]
            s = dot_t(keys_ref[i, 0], qg_ref[n, h, 0])
            gp = dot_t(keys_ref[i, 1], qg_ref[n, h, 1])
            p_parts, d_parts = [], []
            for t in range(2):
                k = NCHUNK * side + 2 * i + t
                part = slice(t * TILE, (t + 1) * TILE)
                shift = lse + 4.0 * far_ref[n, h, k : k + 1, :]
                p = jnp.exp2(s[part] * SCALE2 - shift)
                p_parts.append(p.astype(jnp.bfloat16))
                d_parts.append((p * (gp[part] - delta)).astype(jnp.bfloat16))
            ps.append(jnp.concatenate(p_parts, axis=0))
            d = jnp.concatenate(d_parts, axis=0)
            ds.append(d)
            ds_ref[h, rows] = d
        dv_acc[rows] += dot_n(jnp.concatenate(ps, axis=1), g_all)
        dk_acc[rows] += dot_n(jnp.concatenate(ds, axis=1), q_all)
    used = slice(2 * side * HALF, 2 * (side + 1) * HALF)
    return [dot_n(kt_ref[:, used], ds_ref[h]) for h in range(2)]


def split_keys(core, dk_acc, dv_acc, keep_ref, send_ref):
    rows = pl.ds(core * HALF, HALF)
    keep_ref[0] = dk_acc[rows] * SCALE
    keep_ref[1] = dv_acc[rows]
    rows = pl.ds((1 - core) * HALF, HALF)
    send_ref[0] = (dk_acc[rows] * SCALE).astype(jnp.bfloat16)
    send_ref[1] = dv_acc[rows].astype(jnp.bfloat16)


def there_kernel(
    live_ref,
    qg_ref,
    there_ref,
    far_ref,
    stats_ref,
    kt_ref,
    keep_ref,
    send_ref,
    dqt_ref,
    dk_acc,
    dv_acc,
    ds_ref,
):
    dk_acc[...] = jnp.zeros_like(dk_acc)
    dv_acc[...] = jnp.zeros_like(dv_acc)

    def group(n, carry):
        @pl.when(live_ref[2 * n + 1] > 0)
        def _():
            parts = side_grads(
                1, n, qg_ref, there_ref, far_ref, stats_ref, kt_ref, dk_acc, dv_acc, ds_ref
            )
            for h in range(2):
                dqt_ref[n, h] = parts[h]

        @pl.when(live_ref[2 * n + 1] == 0)
        def _():
            dqt_ref[n] = jnp.zeros((2, HD, HALF), jnp.float32)

        return carry

    lax.fori_loop(0, NX, group, 0)
    split_keys(lax.axis_index("c"), dk_acc, dv_acc, keep_ref, send_ref)


def here_kernel(
    live_ref,
    work_ref,
    qg_ref,
    here_ref,
    far_ref,
    stats_ref,
    kt_ref,
    dqt_ref,
    after_ref,
    keep_ref,
    send_ref,
    dq_ref,
    dk_acc,
    dv_acc,
    ds_ref,
    dq_buf,
    sems,
):
    zh, core, head = (lax.axis_index(name) for name in ("zh", "c", "n"))
    dk_acc[...] = jnp.zeros_like(dk_acc)
    dv_acc[...] = jnp.zeros_like(dv_acc)

    def group(n, carry):
        def deliver(parts):
            for h in range(2):
                dq = (parts[h] * SCALE).T.astype(jnp.bfloat16)
                for t in range(2):
                    slot = jnp.int32(3)
                    for w in range(3):
                        listed = work_ref[4 * n + 2 * zh + core, 4 * head + w]
                        slot = jnp.where(listed == 2 * h + t, w, slot)
                    dq_buf[n, slot] = dq[t * TILE : (t + 1) * TILE]

        @pl.when(live_ref[2 * n] > 0)
        def _():
            parts = side_grads(
                0, n, qg_ref, here_ref, far_ref, stats_ref, kt_ref, dk_acc, dv_acc, ds_ref
            )
            deliver([parts[h] + dqt_ref[n, h] for h in range(2)])

        @pl.when(live_ref[2 * n] == 0)
        def _():
            deliver([dqt_ref[n, h] for h in range(2)])

        pltpu.make_async_copy(dq_buf.at[n], dq_ref.at[n], sems.at[n]).start()
        return carry

    lax.fori_loop(0, NX, group, 0)
    split_keys(core, dk_acc, dv_acc, keep_ref, send_ref)
    for n in range(NX):
        pltpu.make_async_copy(dq_buf.at[n], dq_ref.at[n], sems.at[n]).wait()


VMEM = pl.BlockSpec(memory_space=pltpu.VMEM)
SMEM = pl.BlockSpec(memory_space=pltpu.SMEM)


def flipped(value, axis):
    return lax.ppermute(value, axis, [(0, 1), (1, 0)])


def across(value):
    return lax.ppermute(value, ("zh", "p"), [(0, 3), (1, 2), (2, 1), (3, 0)])


def run_spread(own, mate):
    return pl.pallas_call(
        spread_kernel,
        out_shape=jax.ShapeDtypeStruct((NX, 2) + own.shape, own.dtype),
        in_specs=[VMEM] * 2,
        out_specs=pl.BlockSpec(memory_space=pl.ANY),
        scratch_shapes=[pltpu.SemaphoreType.DMA((2 * NX,))],
        compiler_params=pltpu.CompilerParams(vmem_limit_bytes=8 * 1024 * 1024),
        name="spread",
    )(own, mate)


def run_masks(tiles, after):
    return pl.pallas_call(
        mask_kernel,
        out_shape=[
            jax.ShapeDtypeStruct((NX, 2, 2 * NCHUNK, HALF), jnp.float32),
            jax.ShapeDtypeStruct((2 * NX,), jnp.int32),
        ],
        in_specs=[VMEM, pl.BlockSpec(memory_space=pl.ANY)],
        out_specs=[VMEM, SMEM],
        scratch_shapes=[pltpu.VMEM((2 * NCHUNK, 64, TILE), jnp.float32)],
        compiler_params=pltpu.CompilerParams(vmem_limit_bytes=8 * 1024 * 1024),
        cost_estimate=pl.CostEstimate(flops=10**10, bytes_accessed=2**20, transcendentals=0),
        name="masks",
    )(tiles, after)


def run_stats(live, qg, kv, far):
    return pl.pallas_call(
        stats_kernel,
        out_shape=jax.ShapeDtypeStruct((BLOCKS, NX, 2, 1, 2 * HALF), jnp.float32),
        in_specs=[SMEM] + [VMEM] * 4,
        out_specs=VMEM,
        compiler_params=pltpu.CompilerParams(vmem_limit_bytes=32 * 1024 * 1024),
        cost_estimate=pl.CostEstimate(flops=10**9, bytes_accessed=2**21, transcendentals=2**21),
        name="stats",
    )(live, qg, *kv, far)


def run_turn(kv, after):
    return pl.pallas_call(
        turn_kernel,
        out_shape=jax.ShapeDtypeStruct((HD, NCHUNK * HALF), jnp.bfloat16),
        in_specs=[VMEM, VMEM, pl.BlockSpec(memory_space=pl.ANY)],
        out_specs=VMEM,
        compiler_params=pltpu.CompilerParams(vmem_limit_bytes=8 * 1024 * 1024),
        cost_estimate=pl.CostEstimate(flops=10**9, bytes_accessed=2**20, transcendentals=0),
        name="turn",
    )(*kv, after)


ACCUMULATORS = [
    pltpu.VMEM((2 * HALF, HD), jnp.float32),
    pltpu.VMEM((2 * HALF, HD), jnp.float32),
    pltpu.VMEM((2, 2 * HALF, HALF), jnp.bfloat16),
]


def run_there(live, qg, there, far, stats, kt):
    return pl.pallas_call(
        there_kernel,
        out_shape=[
            jax.ShapeDtypeStruct((2, HALF, HD), jnp.float32),
            jax.ShapeDtypeStruct((2, HALF, HD), jnp.bfloat16),
            jax.ShapeDtypeStruct((NX, 2, HD, HALF), jnp.float32),
        ],
        in_specs=[SMEM] + [VMEM] * 5,
        out_specs=[VMEM] * 3,
        scratch_shapes=ACCUMULATORS,
        compiler_params=pltpu.CompilerParams(vmem_limit_bytes=24 * 1024 * 1024),
        cost_estimate=pl.CostEstimate(flops=10**9, bytes_accessed=2**21, transcendentals=2**20),
        name="there",
    )(live, qg, there, far, stats, kt)


def run_here(live, work, qg, here, far, stats, kt, dqt, after):
    anywhere = pl.BlockSpec(memory_space=pl.ANY)
    return pl.pallas_call(
        here_kernel,
        out_shape=[
            jax.ShapeDtypeStruct((2, HALF, HD), jnp.float32),
            jax.ShapeDtypeStruct((2, HALF, HD), jnp.bfloat16),
            jax.ShapeDtypeStruct((NX, 4, TILE, HD), jnp.bfloat16),
        ],
        in_specs=[SMEM, SMEM] + [VMEM] * 6 + [anywhere],
        out_specs=[VMEM, VMEM, anywhere],
        scratch_shapes=ACCUMULATORS
        + [pltpu.VMEM((NX, 4, TILE, HD), jnp.bfloat16), pltpu.SemaphoreType.DMA((NX,))],
        compiler_params=pltpu.CompilerParams(vmem_limit_bytes=24 * 1024 * 1024),
        cost_estimate=pl.CostEstimate(flops=10**11, bytes_accessed=2**21, transcendentals=2**20),
        name="here",
    )(live, work, qg, here, far, stats, kt, dqt, after)


def finish_kernel(keep_ref, sibling_ref, arrived_ref, dk_ref, dv_ref):
    for i, out_ref in enumerate((dk_ref, dv_ref)):
        total = keep_ref[i] + sibling_ref[i].astype(jnp.float32)
        out_ref[...] = (total + arrived_ref[i].astype(jnp.float32)).astype(jnp.bfloat16)


def run_finish(keep, sibling, arrived):
    return pl.pallas_call(
        finish_kernel,
        out_shape=[jax.ShapeDtypeStruct((HALF, HD), jnp.bfloat16)] * 2,
        in_specs=[VMEM] * 3,
        out_specs=[VMEM] * 2,
        compiler_params=pltpu.CompilerParams(vmem_limit_bytes=8 * 1024 * 1024),
        cost_estimate=pl.CostEstimate(flops=10**11, bytes_accessed=2**20, transcendentals=0),
        name="finish",
    )(keep, sibling, arrived)


def sum_kernel(parts_ref, dq_ref):
    dq = parts_ref[0].astype(jnp.float32)
    for j in range(1, BLOCKS):
        dq = dq + parts_ref[j].astype(jnp.float32)
    dq_ref[...] = dq.astype(jnp.bfloat16)


def run_sum(parts):
    return pl.pallas_call(
        sum_kernel,
        out_shape=jax.ShapeDtypeStruct((HALF, HD), jnp.bfloat16),
        in_specs=[VMEM],
        out_specs=VMEM,
        compiler_params=pltpu.CompilerParams(vmem_limit_bytes=8 * 1024 * 1024),
        name="sum",
    )(parts)


def on_device(queries, keys, values, grad_out, key_tiles, work_lists):
    own_qg = jnp.stack([queries[0, 0], grad_out[0, 0]])
    mate_qg = flipped(own_qg, "p")
    own_kv = jnp.stack([keys[0, 0], values[0, 0]])
    across_kv = across(own_kv)
    spread = run_spread(own_qg, mate_qg)
    all_qg = lax.all_to_all(spread, "x", 0, 0)
    far, live = run_masks(key_tiles, spread)
    own_kv, _ = lax.optimization_barrier((own_kv, far))
    kv = (lax.all_gather(own_kv, "c"), lax.all_gather(across_kv, "c"))
    work = work_lists.reshape(16, 64)

    own_stats = run_stats(live, all_qg, kv, far)
    kt = run_turn(kv, own_stats)
    stats = lax.all_to_all(own_stats, ("x", "p"), 0, 0)
    sibling = 1 - lax.axis_index("c")
    keep_there, send_there, dqt = run_there(live, all_qg, kv[1], far, stats, kt)
    there = lax.dynamic_index_in_dim(lax.all_gather(send_there, "c"), sibling, 0, False)
    dkv_out = (keep_there + there.astype(jnp.float32)).astype(jnp.bfloat16)
    from_across = across(dkv_out)
    keep, send, dq = run_here(live, work, all_qg, kv[0], far, stats, kt, dqt, dkv_out)
    dq_parts = lax.all_to_all(dq.reshape(BLOCKS, HALF, HD), ("x", "p"), 0, 0)
    here = lax.dynamic_index_in_dim(lax.all_gather(send, "c"), sibling, 0, False)
    grad_keys, grad_values = run_finish(keep, here, from_across)
    outs = (run_sum(dq_parts), grad_keys, grad_values)
    return tuple(out[None, None] for out in outs)


def solution(mesh):
    devices = mesh.devices.reshape(4, 2, 2, 16, 2)
    fine = Mesh(devices, ("x", "zh", "c", "n", "p"))
    spec = P(("x", "zh", "c"), ("n", "p"), None, None)
    return jax.shard_map(
        on_device,
        mesh=fine,
        in_specs=(spec, spec, spec, spec, P(), P()),
        out_specs=(spec, spec, spec),
        check_vma=False,
    )
```

```python
import functools

import jax
import jax.numpy as jnp
from jax import lax
from jax.experimental import pallas as pl
from jax.experimental.pallas import tpu as pltpu
from jax.sharding import Mesh, PartitionSpec as P

TILE = 128
HD = 128
HALF = 256
NX = 4
NCHUNK = 4
BLOCKS = 2 * NX
ROWS = BLOCKS * HALF
SCALE = HD**-0.5
SCALE2 = SCALE * 1.4426950408889634
FAR = 1e30


def dot_t(a, b):
    return lax.dot_general(a, b, (((1,), (1,)), ((), ())), preferred_element_type=jnp.float32)


def dot_n(a, b):
    return jnp.dot(a, b, preferred_element_type=jnp.float32)


def spread_kernel(own_ref, mate_ref, out_ref, sems):
    half = lax.axis_index("p")
    copies = []
    for j in range(NX):
        for i, (source, index) in enumerate(((own_ref, half), (mate_ref, 1 - half))):
            target = out_ref.at[j, index]
            copies.append(pltpu.make_async_copy(source, target, sems.at[2 * j + i]))
    for copy in copies:
        copy.start()
    for copy in copies:
        copy.wait()


def mask_kernel(tiles_ref, after_ref, far_ref, live_ref, table_ref):
    x, zh, core, half = (lax.axis_index(name) for name in ("x", "zh", "c", "p"))
    tiles = tiles_ref[...]
    for k in range(2 * NCHUNK):
        chunk_zh = zh if k // 4 == 0 else 1 - zh
        chunk_half = half if k // 4 == 0 else 1 - half
        key_id = (4 * x + 2 * chunk_zh + k // 2 % 2) * 4 + 2 * chunk_half + k % 2
        hit = jnp.where(tiles == key_id, 0.0, FAR)
        table_ref[k] = jnp.broadcast_to(jnp.min(hit, axis=1, keepdims=True), (64, TILE))
    for n in range(NX):
        first = (4 * n + 2 * zh + core) * 4
        for side in range(2):
            nearest = jnp.full((4, TILE), FAR, jnp.float32)
            for k in range(NCHUNK * side, NCHUNK * (side + 1)):
                four = table_ref[k, pl.ds(first, 4), :]
                nearest = jnp.minimum(nearest, four)
                for h in range(2):
                    far_ref[n, h, k : k + 1, :TILE] = four[2 * h : 2 * h + 1]
                    far_ref[n, h, k : k + 1, TILE:] = four[2 * h + 1 : 2 * h + 2]
            live_ref[2 * n + side] = (jnp.min(nearest) < 1.0).astype(jnp.int32)


def by_sides(live_ref, n, work, nothing):
    here, there = live_ref[2 * n], live_ref[2 * n + 1]
    pl.when((here > 0) & (there > 0))(lambda: work((0, 1, 2, 3)))
    pl.when((here > 0) & (there == 0))(lambda: work((0, 1)))
    pl.when((here == 0) & (there > 0))(lambda: work((2, 3)))
    pl.when((here == 0) & (there == 0))(nothing)


def stats_kernel(live_ref, qg_ref, here_ref, there_ref, far_ref, out_ref, buf, sems):
    chunks = (here_ref.at[0], here_ref.at[1], there_ref.at[0], there_ref.at[1])

    def group(n, carry):
        def work(subset):
            for h in range(2):
                q = qg_ref[n, h, 0]
                g = qg_ref[n, h, 1]
                far = far_ref[n, h]
                scores = {}
                top = jnp.full((1, HALF), -FAR, jnp.float32)
                for i in subset:
                    s = dot_t(chunks[i][0], q)
                    for t in range(2):
                        k = 2 * i + t
                        scores[k] = s[t * TILE : (t + 1) * TILE]
                        near = jnp.max(scores[k], axis=0, keepdims=True) - far[k : k + 1]
                        top = jnp.maximum(top, near)
                top = top * SCALE2
                total = jnp.zeros((1, HALF), jnp.float32)
                weighted = jnp.zeros((1, HALF), jnp.float32)
                for i in subset:
                    gp = dot_t(chunks[i][1], g)
                    for t in range(2):
                        k = 2 * i + t
                        e = jnp.exp2(scores[k] * SCALE2 - (top + 4.0 * far[k : k + 1]))
                        total = total + jnp.sum(e, axis=0, keepdims=True)
                        weighted = weighted + jnp.sum(
                            e * gp[t * TILE : (t + 1) * TILE], axis=0, keepdims=True
                        )
                some = total > 0.0
                safe = jnp.where(some, total, 1.0)
                lse = jnp.where(some, top + jnp.log2(safe), -FAR)
                mean = jnp.where(some, weighted / safe, 0.0)
                buf[n, h, :, :HALF] = lse
                buf[n, h, :, HALF:] = mean

        def nothing():
            for h in range(2):
                buf[n, h, :, :HALF] = jnp.full((1, HALF), -FAR, jnp.float32)
                buf[n, h, :, HALF:] = jnp.zeros((1, HALF), jnp.float32)

        by_sides(live_ref, n, work, nothing)
        for j in range(BLOCKS):
            pltpu.make_async_copy(buf.at[n], out_ref.at[j, n], sems.at[n, j]).start()
        return carry

    lax.fori_loop(0, NX, group, 0)
    for n in range(NX):
        for j in range(BLOCKS):
            pltpu.make_async_copy(buf.at[n], out_ref.at[j, n], sems.at[n, j]).wait()


def turn_kernel(here_ref, there_ref, after_ref, kt_ref):
    chunks = (here_ref.at[0], here_ref.at[1], there_ref.at[0], there_ref.at[1])
    for i, chunk in enumerate(chunks):
        kt_ref[:, i * HALF : (i + 1) * HALF] = chunk[0].T


def side_grads(side, n, qg_ref, keys_ref, far_ref, stats_ref, kt_ref, dk_acc, dv_acc, ds_ref):
    q_all = qg_ref[n, :, 0].reshape(2 * HALF, HD)
    g_all = qg_ref[n, :, 1].reshape(2 * HALF, HD)
    rows_stats = []
    for h in range(2):
        lse_parts = [stats_ref[j, n, h, :, :HALF] for j in range(BLOCKS)]
        top = functools.reduce(jnp.maximum, lse_parts)
        total = jnp.zeros((1, HALF), jnp.float32)
        weighted = jnp.zeros((1, HALF), jnp.float32)
        for j in range(BLOCKS):
            w = jnp.exp2(lse_parts[j] - top)
            total = total + w
            weighted = weighted + w * stats_ref[j, n, h, :, HALF:]
        rows_stats.append((top + jnp.log2(total), weighted / total))
    for i in range(2):
        rows = slice(i * HALF, (i + 1) * HALF)
        ps, ds = [], []
        for h in range(2):
            lse, delta = rows_stats[h]
            s = dot_t(keys_ref[i, 0], qg_ref[n, h, 0])
            gp = dot_t(keys_ref[i, 1], qg_ref[n, h, 1])
            p_parts, d_parts = [], []
            for t in range(2):
                k = NCHUNK * side + 2 * i + t
                part = slice(t * TILE, (t + 1) * TILE)
                shift = lse + 4.0 * far_ref[n, h, k : k + 1, :]
                p = jnp.exp2(s[part] * SCALE2 - shift)
                p_parts.append(p.astype(jnp.bfloat16))
                d_parts.append((p * (gp[part] - delta)).astype(jnp.bfloat16))
            ps.append(jnp.concatenate(p_parts, axis=0))
            d = jnp.concatenate(d_parts, axis=0)
            ds.append(d)
            ds_ref[h, rows] = d
        dv_acc[rows] += dot_n(jnp.concatenate(ps, axis=1), g_all)
        dk_acc[rows] += dot_n(jnp.concatenate(ds, axis=1), q_all)
    used = slice(2 * side * HALF, 2 * (side + 1) * HALF)
    return [dot_n(kt_ref[:, used], ds_ref[h]) for h in range(2)]


def split_keys(core, dk_acc, dv_acc, keep_ref, send_ref):
    rows = pl.ds(core * HALF, HALF)
    keep_ref[0] = dk_acc[rows] * SCALE
    keep_ref[1] = dv_acc[rows]
    rows = pl.ds((1 - core) * HALF, HALF)
    send_ref[0] = (dk_acc[rows] * SCALE).astype(jnp.bfloat16)
    send_ref[1] = dv_acc[rows].astype(jnp.bfloat16)


def there_kernel(
    live_ref,
    qg_ref,
    there_ref,
    far_ref,
    stats_ref,
    kt_ref,
    keep_ref,
    send_ref,
    dqt_ref,
    dk_acc,
    dv_acc,
    ds_ref,
):
    dk_acc[...] = jnp.zeros_like(dk_acc)
    dv_acc[...] = jnp.zeros_like(dv_acc)

    def group(n, carry):
        @pl.when(live_ref[2 * n + 1] > 0)
        def _():
            parts = side_grads(
                1, n, qg_ref, there_ref, far_ref, stats_ref, kt_ref, dk_acc, dv_acc, ds_ref
            )
            for h in range(2):
                dqt_ref[n, h] = parts[h]

        @pl.when(live_ref[2 * n + 1] == 0)
        def _():
            dqt_ref[n] = jnp.zeros((2, HD, HALF), jnp.float32)

        return carry

    lax.fori_loop(0, NX, group, 0)
    split_keys(lax.axis_index("c"), dk_acc, dv_acc, keep_ref, send_ref)


def here_kernel(
    live_ref,
    work_ref,
    qg_ref,
    here_ref,
    far_ref,
    stats_ref,
    kt_ref,
    dqt_ref,
    after_ref,
    keep_ref,
    send_ref,
    dq_ref,
    dk_acc,
    dv_acc,
    ds_ref,
    dq_buf,
    sems,
):
    zh, core, head = (lax.axis_index(name) for name in ("zh", "c", "n"))
    dk_acc[...] = jnp.zeros_like(dk_acc)
    dv_acc[...] = jnp.zeros_like(dv_acc)

    def group(n, carry):
        def deliver(parts):
            for h in range(2):
                dq = (parts[h] * SCALE).T.astype(jnp.bfloat16)
                for t in range(2):
                    slot = jnp.int32(3)
                    for w in range(3):
                        listed = work_ref[4 * n + 2 * zh + core, 4 * head + w]
                        slot = jnp.where(listed == 2 * h + t, w, slot)
                    dq_buf[n, slot] = dq[t * TILE : (t + 1) * TILE]

        @pl.when(live_ref[2 * n] > 0)
        def _():
            parts = side_grads(
                0, n, qg_ref, here_ref, far_ref, stats_ref, kt_ref, dk_acc, dv_acc, ds_ref
            )
            deliver([parts[h] + dqt_ref[n, h] for h in range(2)])

        @pl.when(live_ref[2 * n] == 0)
        def _():
            deliver([dqt_ref[n, h] for h in range(2)])

        pltpu.make_async_copy(dq_buf.at[n], dq_ref.at[n], sems.at[n]).start()
        return carry

    lax.fori_loop(0, NX, group, 0)
    split_keys(core, dk_acc, dv_acc, keep_ref, send_ref)
    for n in range(NX):
        pltpu.make_async_copy(dq_buf.at[n], dq_ref.at[n], sems.at[n]).wait()


VMEM = pl.BlockSpec(memory_space=pltpu.VMEM)
SMEM = pl.BlockSpec(memory_space=pltpu.SMEM)


def flipped(value, axis):
    return lax.ppermute(value, axis, [(0, 1), (1, 0)])


def across(value):
    return lax.ppermute(value, ("zh", "p"), [(0, 3), (1, 2), (2, 1), (3, 0)])


def run_spread(own, mate):
    return pl.pallas_call(
        spread_kernel,
        out_shape=jax.ShapeDtypeStruct((NX, 2) + own.shape, own.dtype),
        in_specs=[VMEM] * 2,
        out_specs=pl.BlockSpec(memory_space=pl.ANY),
        scratch_shapes=[pltpu.SemaphoreType.DMA((2 * NX,))],
        compiler_params=pltpu.CompilerParams(vmem_limit_bytes=8 * 1024 * 1024),
        name="spread",
    )(own, mate)


def run_masks(tiles, after):
    return pl.pallas_call(
        mask_kernel,
        out_shape=[
            jax.ShapeDtypeStruct((NX, 2, 2 * NCHUNK, HALF), jnp.float32),
            jax.ShapeDtypeStruct((2 * NX,), jnp.int32),
        ],
        in_specs=[VMEM, pl.BlockSpec(memory_space=pl.ANY)],
        out_specs=[VMEM, SMEM],
        scratch_shapes=[pltpu.VMEM((2 * NCHUNK, 64, TILE), jnp.float32)],
        compiler_params=pltpu.CompilerParams(vmem_limit_bytes=8 * 1024 * 1024),
        cost_estimate=pl.CostEstimate(flops=10**10, bytes_accessed=2**20, transcendentals=0),
        name="masks",
    )(tiles, after)


def run_stats(live, qg, kv, far):
    return pl.pallas_call(
        stats_kernel,
        out_shape=jax.ShapeDtypeStruct((BLOCKS, NX, 2, 1, 2 * HALF), jnp.float32),
        in_specs=[SMEM] + [VMEM] * 4,
        out_specs=pl.BlockSpec(memory_space=pl.ANY),
        scratch_shapes=[
            pltpu.VMEM((NX, 2, 1, 2 * HALF), jnp.float32),
            pltpu.SemaphoreType.DMA((NX, BLOCKS)),
        ],
        compiler_params=pltpu.CompilerParams(vmem_limit_bytes=32 * 1024 * 1024),
        cost_estimate=pl.CostEstimate(flops=10**9, bytes_accessed=2**21, transcendentals=2**21),
        name="stats",
    )(live, qg, *kv, far)


def run_turn(kv, after):
    return pl.pallas_call(
        turn_kernel,
        out_shape=jax.ShapeDtypeStruct((HD, NCHUNK * HALF), jnp.bfloat16),
        in_specs=[VMEM, VMEM, pl.BlockSpec(memory_space=pl.ANY)],
        out_specs=VMEM,
        compiler_params=pltpu.CompilerParams(vmem_limit_bytes=8 * 1024 * 1024),
        cost_estimate=pl.CostEstimate(flops=10**9, bytes_accessed=2**20, transcendentals=0),
        name="turn",
    )(*kv, after)


ACCUMULATORS = [
    pltpu.VMEM((2 * HALF, HD), jnp.float32),
    pltpu.VMEM((2 * HALF, HD), jnp.float32),
    pltpu.VMEM((2, 2 * HALF, HALF), jnp.bfloat16),
]


def run_there(live, qg, there, far, stats, kt):
    return pl.pallas_call(
        there_kernel,
        out_shape=[
            jax.ShapeDtypeStruct((2, HALF, HD), jnp.float32),
            jax.ShapeDtypeStruct((2, HALF, HD), jnp.bfloat16),
            jax.ShapeDtypeStruct((NX, 2, HD, HALF), jnp.float32),
        ],
        in_specs=[SMEM] + [VMEM] * 5,
        out_specs=[VMEM] * 3,
        scratch_shapes=ACCUMULATORS,
        compiler_params=pltpu.CompilerParams(vmem_limit_bytes=24 * 1024 * 1024),
        cost_estimate=pl.CostEstimate(flops=10**9, bytes_accessed=2**21, transcendentals=2**20),
        name="there",
    )(live, qg, there, far, stats, kt)


def run_here(live, work, qg, here, far, stats, kt, dqt, after):
    anywhere = pl.BlockSpec(memory_space=pl.ANY)
    return pl.pallas_call(
        here_kernel,
        out_shape=[
            jax.ShapeDtypeStruct((2, HALF, HD), jnp.float32),
            jax.ShapeDtypeStruct((2, HALF, HD), jnp.bfloat16),
            jax.ShapeDtypeStruct((NX, 4, TILE, HD), jnp.bfloat16),
        ],
        in_specs=[SMEM, SMEM] + [VMEM] * 6 + [anywhere],
        out_specs=[VMEM, VMEM, anywhere],
        scratch_shapes=ACCUMULATORS
        + [pltpu.VMEM((NX, 4, TILE, HD), jnp.bfloat16), pltpu.SemaphoreType.DMA((NX,))],
        compiler_params=pltpu.CompilerParams(vmem_limit_bytes=24 * 1024 * 1024),
        cost_estimate=pl.CostEstimate(flops=10**11, bytes_accessed=2**21, transcendentals=2**20),
        name="here",
    )(live, work, qg, here, far, stats, kt, dqt, after)


def finish_kernel(keep_ref, sibling_ref, arrived_ref, dk_ref, dv_ref):
    for i, out_ref in enumerate((dk_ref, dv_ref)):
        total = keep_ref[i] + sibling_ref[i].astype(jnp.float32)
        out_ref[...] = (total + arrived_ref[i].astype(jnp.float32)).astype(jnp.bfloat16)


def run_finish(keep, sibling, arrived):
    return pl.pallas_call(
        finish_kernel,
        out_shape=[jax.ShapeDtypeStruct((HALF, HD), jnp.bfloat16)] * 2,
        in_specs=[VMEM] * 3,
        out_specs=[VMEM] * 2,
        compiler_params=pltpu.CompilerParams(vmem_limit_bytes=8 * 1024 * 1024),
        cost_estimate=pl.CostEstimate(flops=10**11, bytes_accessed=2**20, transcendentals=0),
        name="finish",
    )(keep, sibling, arrived)


def sum_kernel(parts_ref, dq_ref):
    dq = parts_ref[0].astype(jnp.float32)
    for j in range(1, BLOCKS):
        dq = dq + parts_ref[j].astype(jnp.float32)
    dq_ref[...] = dq.astype(jnp.bfloat16)


def run_sum(parts):
    return pl.pallas_call(
        sum_kernel,
        out_shape=jax.ShapeDtypeStruct((HALF, HD), jnp.bfloat16),
        in_specs=[VMEM],
        out_specs=VMEM,
        compiler_params=pltpu.CompilerParams(vmem_limit_bytes=8 * 1024 * 1024),
        name="sum",
    )(parts)


def on_device(queries, keys, values, grad_out, key_tiles, work_lists):
    own_qg = jnp.stack([queries[0, 0], grad_out[0, 0]])
    mate_qg = flipped(own_qg, "p")
    own_kv = jnp.stack([keys[0, 0], values[0, 0]])
    across_kv = across(own_kv)
    spread = run_spread(own_qg, mate_qg)
    all_qg = lax.all_to_all(spread, "x", 0, 0)
    far, live = run_masks(key_tiles, spread)
    own_kv, _ = lax.optimization_barrier((own_kv, far))
    kv = (lax.all_gather(own_kv, "c"), lax.all_gather(across_kv, "c"))
    work = work_lists.reshape(16, 64)

    own_stats = run_stats(live, all_qg, kv, far)
    kt = run_turn(kv, own_stats)
    stats = lax.all_to_all(own_stats, ("x", "p"), 0, 0)
    sibling = 1 - lax.axis_index("c")
    keep_there, send_there, dqt = run_there(live, all_qg, kv[1], far, stats, kt)
    there = lax.dynamic_index_in_dim(lax.all_gather(send_there, "c"), sibling, 0, False)
    dkv_out = (keep_there + there.astype(jnp.float32)).astype(jnp.bfloat16)
    from_across = across(dkv_out)
    keep, send, dq = run_here(live, work, all_qg, kv[0], far, stats, kt, dqt, dkv_out)
    dq_parts = lax.all_to_all(dq.reshape(BLOCKS, HALF, HD), ("x", "p"), 0, 0)
    here = lax.dynamic_index_in_dim(lax.all_gather(send, "c"), sibling, 0, False)
    grad_keys, grad_values = run_finish(keep, here, from_across)
    outs = (run_sum(dq_parts), grad_keys, grad_values)
    return tuple(out[None, None] for out in outs)


def solution(mesh):
    devices = mesh.devices.reshape(4, 2, 2, 16, 2)
    fine = Mesh(devices, ("x", "zh", "c", "n", "p"))
    spec = P(("x", "zh", "c"), ("n", "p"), None, None)
    return jax.shard_map(
        on_device,
        mesh=fine,
        in_specs=(spec, spec, spec, spec, P(), P()),
        out_specs=(spec, spec, spec),
        check_vma=False,
    )
```
